256 devices in a mesh: outer: 16 (over x, z_lo, core), inner: 16 (over y, z_hi).
Axes of the slice: x: 4, y: 4, z: 8 (z_hi: 4, z_lo: 2; z = z_hi * 2 + z_lo), core: 2. Of those that a mesh axis runs over, the one named last changes fastest.
Arguments:
- queries: bfloat16 [32768, 512], P(('outer', 'inner')), may hold values from -1.5 to 1.5
- key_rows: bfloat16 [32768, 128], P(('outer', 'inner')), may hold values from -1.5 to 1.5
- value_rows: bfloat16 [32768, 128], P(('outer', 'inner')), may hold values from -6 to 6
- forward_out: bfloat16 [32768, 512], P(('outer', 'inner')), may hold values from -6 to 6
- out_grad: bfloat16 [32768, 512], P(('outer', 'inner')), may hold values from -12 to 12
- log_norm: bfloat16 [32768, 4], P(('outer', 'inner')), may hold values from -1 to 14, as said below
Outputs:
- query_grad: bfloat16 [32768, 512], P(('outer', 'inner'))
- key_grad: bfloat16 [32768, 128], P(('outer', 'inner'))
- value_grad: bfloat16 [32768, 128], P(('outer', 'inner'))
The draws below stay inside these ranges and needn't reach their ends.
Inputs may be any that keep to these rules, and one draw needn't show every extreme that they name: log_norm[t, h] is log(t + 1) plus a term between -0.2 and 0.8, so each row's weights sum to about one.
All inputs are finite; a program needn't handle non-finite values.
Results may differ from the reference program's by a relative error of at most 0.02.
Values may be sent and summed in bfloat16 or wider, within the bound.
A program may use at most 64 MiB of HBM per device.

```python
import jax
import jax.numpy as jnp
from jax import lax

HEADS = 4
HEAD_DIM = 128
TOKENS = 32768


def draw_log_norm(key, part):
    key = jax.random.fold_in(key, 11)
    positions = jnp.arange(TOKENS, dtype=jnp.float32)[:, None]
    noise = jax.random.uniform(key, (TOKENS, HEADS), jnp.float32, -0.5, 0.5)
    return (jnp.log(positions + 1.0) + 0.3 + noise).astype(jnp.bfloat16)


def block_scale(rng, dims, shards, smallest, high):
    level = 1.0
    for axis_at, blocks in shards:
        draws = jax.random.uniform(jax.random.fold_in(jax.random.fold_in(rng, 6), axis_at), (blocks,), jnp.float32, smallest / len(shards), high / len(shards))
        level = level * jnp.repeat(jnp.exp(draws), dims[axis_at] // blocks).reshape((-1,) + (1,) * (len(dims) - 1 - axis_at))
    return level


def normal_values(own_key, dims, width, bound, pieces=(), held_as=jnp.bfloat16):
    array = width * jax.random.normal(own_key, dims, jnp.float32)
    if pieces:
        array = array * block_scale(own_key, dims, pieces, -0.22, 0.18)
    return jnp.clip(array, -bound, bound).astype(held_as)


def setup_inputs(seed: int = 0) -> dict:
    splits = jax.random.split(jax.random.key(seed), 7)
    return {
        "queries": jnp.clip(jax.random.uniform(splits[0], (TOKENS, HEADS * HEAD_DIM), jnp.float32, -1.5, 1.5) * block_scale(splits[0], (TOKENS, HEADS * HEAD_DIM), ((0, 256),), -0.4, 0.0), -1.5, 1.5).astype(jnp.bfloat16),
        "key_rows": jnp.clip(jax.random.uniform(splits[1], (TOKENS, HEAD_DIM), jnp.float32, -1.5, 1.5) * block_scale(splits[1], (TOKENS, HEAD_DIM), ((0, 256),), -0.4, 0.0), -1.5, 1.5).astype(jnp.bfloat16),
        "value_rows": normal_values(splits[2], (TOKENS, HEAD_DIM), 1.0, 6.0, ((0, 256),)),
        "forward_out": normal_values(splits[3], (TOKENS, HEADS * HEAD_DIM), 1.0, 6.0, ((0, 256),)),
        "out_grad": normal_values(splits[4], (TOKENS, HEADS * HEAD_DIM), 2.0, 12.0, ((0, 256),)),
        "log_norm": draw_log_norm(jax.random.fold_in(splits[6], 71), 0),
    }


def tile_terms(query_tile, grad_tile, norm_tile, delta_tile, key_tile, value_tile, query_pos, key_pos, scaling):
    scores = jnp.einsum("qhd,kd->hqk", query_tile, key_tile) * scaling
    visible = query_pos[:, None] >= key_pos[None, :]
    weights = jnp.where(visible[None], jnp.exp(scores - norm_tile.T[:, :, None]), 0.0)
    weights_low = lax.optimization_barrier(weights.astype(jnp.bfloat16)).astype(jnp.float32)
    grad_probs = jnp.einsum("qhd,kd->hqk", grad_tile, value_tile)
    grad_scores = weights * (grad_probs - delta_tile.T[:, :, None])
    grad_low = lax.optimization_barrier(grad_scores.astype(jnp.bfloat16)).astype(jnp.float32)
    value_term = jnp.einsum("hqk,qhd->kd", weights_low, grad_tile)
    key_term = jnp.einsum("hqk,qhd->kd", grad_low, query_tile) * scaling
    query_term = jnp.einsum("hqk,kd->qhd", grad_low, key_tile) * scaling
    return query_term, key_term, value_term


def reference(queries, key_rows, value_rows, forward_out, out_grad, log_norm):
    total_rows = queries.shape[0]
    scaling = HEAD_DIM ** -0.5
    query_all = queries.astype(jnp.float32).reshape(total_rows, HEADS, HEAD_DIM)
    grad_all = out_grad.astype(jnp.float32).reshape(total_rows, HEADS, HEAD_DIM)
    output_all = forward_out.astype(jnp.float32).reshape(total_rows, HEADS, HEAD_DIM)
    delta_rows = jnp.sum(grad_all * output_all, axis=2).astype(jnp.bfloat16)
    delta_all = delta_rows.astype(jnp.float32)
    norm_all = log_norm.astype(jnp.float32)
    key_all = key_rows.astype(jnp.float32)
    value_all = value_rows.astype(jnp.float32)
    query_block = min(512, total_rows)
    key_block = min(1024, total_rows)

    def over_queries(accum, block_index):
        key_sum, value_sum = accum
        query_start = (block_index * query_block).astype(jnp.int32)
        query_tile = lax.dynamic_slice_in_dim(query_all, query_start, query_block, 0)
        grad_tile = lax.dynamic_slice_in_dim(grad_all, query_start, query_block, 0)
        norm_tile = lax.dynamic_slice_in_dim(norm_all, query_start, query_block, 0)
        delta_tile = lax.dynamic_slice_in_dim(delta_all, query_start, query_block, 0)
        query_pos = query_start + jnp.arange(query_block, dtype=jnp.int32)

        def over_keys(key_index, running):
            key_start = (key_index * key_block).astype(jnp.int32)

            def active(current):
                query_acc, key_sum, value_sum = current
                key_tile = lax.dynamic_slice_in_dim(key_all, key_start, key_block, 0)
                value_tile = lax.dynamic_slice_in_dim(value_all, key_start, key_block, 0)
                key_pos = key_start + jnp.arange(key_block, dtype=jnp.int32)
                query_term, key_term, value_term = tile_terms(query_tile, grad_tile, norm_tile, delta_tile, key_tile, value_tile, query_pos, key_pos, scaling)
                key_old = lax.dynamic_slice_in_dim(key_sum, key_start, key_block, 0)
                value_old = lax.dynamic_slice_in_dim(value_sum, key_start, key_block, 0)
                key_sum = lax.dynamic_update_slice_in_dim(key_sum, key_old + key_term, key_start, 0)
                value_sum = lax.dynamic_update_slice_in_dim(value_sum, value_old + value_term, key_start, 0)
                return query_acc + query_term, key_sum, value_sum

            return lax.cond(key_start <= query_start + query_block - 1, active, lambda current: current, running)

        start_acc = jnp.zeros((query_block, HEADS, HEAD_DIM), jnp.float32)
        query_acc, key_sum, value_sum = lax.fori_loop(0, total_rows // key_block, over_keys, (start_acc, key_sum, value_sum))
        return (key_sum, value_sum), query_acc

    blocks = jnp.arange(total_rows // query_block, dtype=jnp.int32)
    zero_rows = jnp.zeros((total_rows, HEAD_DIM), jnp.float32)
    (key_sum, value_sum), query_parts = lax.scan(over_queries, (zero_rows, zero_rows), blocks)
    query_grad = query_parts.reshape(total_rows, HEADS * HEAD_DIM).astype(jnp.bfloat16)
    return query_grad, key_sum.astype(jnp.bfloat16), value_sum.astype(jnp.bfloat16)
```

```python
import functools

import jax
import jax.numpy as jnp
import numpy as np
from jax import lax
from jax.experimental import pallas as pl
from jax.experimental.pallas import tpu as pltpu
from jax.sharding import PartitionSpec as P

F32 = jnp.float32
BF16 = jnp.bfloat16
MESH = pl.DeviceIdType.MESH
HEADS = 4
WIDTH = 128
ROWS = 128
HALF = 64
ROOT = float(np.sqrt(128.0))
SCALE = float(1.0 / np.sqrt(128.0))
EXP2_SCALE = float(np.log2(np.e) / np.sqrt(128.0))
NT = (((1,), (1,)), ((), ()))
NN = (((1,), (0,)), ((), ()))
TN = (((0,), (0,)), ((), ()))

dot = functools.partial(lax.dot_general, preferred_element_type=F32)


def attention_grads(
    q_in, k_in, v_in, fo_in, og_in, ln_in,
    dq_out, dk_out, dv_out,
    units, kv, kv_own, acc, dq_acc, sib_out, sib_in, own_out, own_in,
    y_out, y_in, z_out, z_in,
    q_send, q_recv, f_send, f_recv, kz_send, kz_recv, ky_send, ky_recv,
    s_send, s_recv, o_send, o_recv, gy_send, gy_recv, gz_send, gz_recv,
):
    o = lax.axis_index("outer")
    i = lax.axis_index("inner")
    chip = o // 2
    core = o % 2
    x = o // 4
    zl = chip % 2
    y = i // 4
    zh = i % 4
    sibling = (2 * chip + 1 - core, i)
    far = y >= 2
    z_plane = jnp.where(far, 15 - o, o)

    def floor_of(c):
        return jnp.minimum(c, 7 - c)

    own_floor = floor_of(chip)

    def partner(k):
        flip_z = (k == 1) | (k == 4) | (k == 5) | (k == 7)
        one = (k == 2) | (k == 4)
        three = (k == 3) | (k == 5)
        two = k >= 6
        x_one = x + 1 - 2 * (x % 2)
        x_two = jnp.where(x >= 2, x - 2, x + 2)
        xp = jnp.where(one, x_one, jnp.where(three, 3 - x, jnp.where(two, x_two, x)))
        zp = jnp.where(flip_z, 1 - zl, zl)
        return 2 * xp + zp

    chips = [partner(jnp.int32(k)) for k in range(8)]

    def z_peer(d):
        return (z_plane, 4 * y + (zh + d) % 4)

    def y_peer(d):
        return (o, 4 * ((y + d) % 4) + zh)

    barrier = pltpu.get_barrier_semaphore()

    def greet(dev):
        pl.semaphore_signal(barrier, inc=1, device_id=dev, device_id_type=MESH)

    for k in range(1, 8):
        greet((2 * chips[k] + core, i))
    greet(sibling)
    for d in range(1, 4):
        greet(z_peer(d))
        greet(y_peer(d))

    @pl.when(far)
    def _():
        greet(z_peer(0))

    kv_own[0] = k_in[...].reshape(2, HALF, WIDTH)
    kv_own[1] = v_in[...].reshape(2, HALF, WIDTH)
    lane = lax.broadcasted_iota(jnp.int32, (ROWS, WIDTH), 1)
    stat = jnp.zeros((ROWS, WIDTH), F32)
    for h in range(HEADS):
        cols = slice(WIDTH * h, WIDTH * (h + 1))
        shift = ln_in[:, h : h + 1].astype(F32) * (-ROOT)
        high = shift.astype(BF16).astype(F32)
        rest = shift - high
        mid = rest.astype(BF16).astype(F32)
        low = rest - mid
        delta = jnp.sum(
            og_in[:, cols].astype(F32) * fo_in[:, cols].astype(F32), axis=1, keepdims=True
        ).astype(BF16).astype(F32)
        for at, column in ((4 * h, high), (4 * h + 1, mid), (4 * h + 2, low), (64 + h, -delta)):
            stat = jnp.where(lane == at, column, stat)
    units[chip, core, :, 0:512] = q_in[...]
    units[chip, core, :, 512:1024] = og_in[...]
    units[chip, core, :, 1024:1152] = stat.astype(BF16)
    kv[:, :, :, :, WIDTH:] = jnp.ones((2, 2, 16, HALF, WIDTH), BF16)
    acc[...] = jnp.zeros_like(acc)
    dq_acc[...] = jnp.zeros_like(dq_acc)

    @pl.when(jnp.logical_not(far))
    def _():
        kv[:, :, i, :, 0:WIDTH] = kv_own[...]

    pl.semaphore_wait(barrier, jnp.where(far, 15, 14))

    def key_z(s, d):
        return pltpu.make_async_remote_copy(
            src_ref=kv_own.at[:, s],
            dst_ref=kv.at[:, s, i, :, pl.ds(0, WIDTH)],
            send_sem=kz_send.at[s, d],
            recv_sem=kz_recv.at[s, d],
            device_id=z_peer(d),
            device_id_type=MESH,
        )

    def key_y(s, d):
        part = kv.at[:, s, pl.ds(4 * y, 4), :, pl.ds(0, WIDTH)]
        return pltpu.make_async_remote_copy(
            src_ref=part,
            dst_ref=part,
            send_sem=ky_send.at[s, d - 1],
            recv_sem=ky_recv.at[s, d - 1],
            device_id=y_peer(d),
            device_id_type=MESH,
        )

    def start_key_z(s):
        for d in range(1, 4):
            key_z(s, d).start()

        @pl.when(far)
        def _():
            key_z(s, 0).start()

    def wait_key_z(s):
        for d in range(1, 4):
            key_z(s, d).wait_recv()

        @pl.when(far)
        def _():
            key_z(s, 0).wait_recv()

    start_key_z(0)
    start_key_z(1)

    def query_copy(k):
        return pltpu.make_async_remote_copy(
            src_ref=units.at[chip, core],
            dst_ref=units.at[chip, core],
            send_sem=q_send.at[k],
            recv_sem=q_recv.at[k],
            device_id=(2 * partner(k) + core, i),
            device_id_type=MESH,
        )

    def forward_copy(k):
        part = units.at[partner(k), core]
        return pltpu.make_async_remote_copy(
            src_ref=part,
            dst_ref=part,
            send_sem=f_send.at[k],
            recv_sem=f_recv.at[k],
            device_id=sibling,
            device_id_type=MESH,
        )

    forward_copy(0).start()
    for k in range(1, 8):

        @pl.when(chip >= floor_of(chips[k]))
        def _(k=k):
            query_copy(k).start()

    wait_key_z(0)
    for d in range(1, 4):
        key_y(0, d).start()
    wait_key_z(1)
    for d in range(1, 4):
        key_y(1, d).start()
    forward_copy(0).wait_recv()
    for d in range(1, 4):
        key_y(0, d).wait_recv()

    def unit_rows(c, u, base):
        return jnp.concatenate(
            [units[c, u, :, base + WIDTH * h : base + WIDTH * (h + 1)] for h in range(HEADS)],
            axis=0,
        )

    def unit_stats(c, u, first):
        st = units[c, u, :, 1024:1152]
        ln = lax.broadcasted_iota(jnp.int32, (ROWS, WIDTH), 1)
        if first:
            keep = [ln // 4 == h for h in range(HEADS)]
        else:
            keep = [ln == 64 + h for h in range(HEADS)]
        return jnp.concatenate([jnp.where(m, st, jnp.zeros_like(st)) for m in keep], axis=0)

    def tile(c, cores, s, half, plane, masked):
        keys = pl.ds(8 * half, 8)
        k = kv[0, s, keys].reshape(8 * HALF, 2 * WIDTH)
        v = kv[1, s, keys].reshape(8 * HALF, 2 * WIDTH)
        q = jnp.concatenate([unit_rows(c, u, 0) for u in cores], axis=0)
        g = jnp.concatenate([unit_rows(c, u, 512) for u in cores], axis=0)
        q_stat = jnp.concatenate([unit_stats(c, u, True) for u in cores], axis=0)
        g_stat = jnp.concatenate([unit_stats(c, u, False) for u in cores], axis=0)
        scores = dot(k, jnp.concatenate([q, q_stat], axis=1), NT)
        probs = dot(v, jnp.concatenate([g, g_stat], axis=1), NT)
        w = jnp.exp2(scores * EXP2_SCALE)
        if masked:
            row = lax.broadcasted_iota(jnp.int32, (8 * HALF, 1), 0)
            col = lax.broadcasted_iota(jnp.int32, (1, HEADS * ROWS), 1)
            key_pos = (plane * 16 + 8 * half) * ROWS + s * HALF + (row // HALF) * ROWS + row % HALF
            query_pos = ((2 * c + cores[0]) * 16 + i) * ROWS + col % ROWS
            w = jnp.where(key_pos <= query_pos, w, 0.0)
        gs = (w * probs).astype(BF16)
        w = w.astype(BF16)
        acc[s, 0, keys] += dot(gs, q, NN).reshape(8, HALF, WIDTH)
        acc[s, 1, keys] += dot(w, g, NN).reshape(8, HALF, WIDTH)
        dq = dot(gs, k[:, 0:WIDTH], TN)
        for n, u in enumerate(cores):
            dq_acc[c, u] += dq[512 * n : 512 * (n + 1)]

    def sibling_copy(k):
        return pltpu.make_async_remote_copy(
            src_ref=sib_out.at[k],
            dst_ref=sib_in.at[k],
            send_sem=s_send.at[k],
            recv_sem=s_recv.at[k],
            device_id=sibling,
            device_id_type=MESH,
        )

    def owner_copy(k):
        return pltpu.make_async_remote_copy(
            src_ref=own_out.at[k],
            dst_ref=own_in.at[k],
            send_sem=o_send.at[k],
            recv_sem=o_recv.at[k],
            device_id=(2 * partner(k) + core, i),
            device_id_type=MESH,
        )

    def give_sibling(k):
        c = partner(k)

        @pl.when(c >= own_floor)
        def _():
            sib_out[k] = dq_acc[c, 1 - core].astype(BF16)
            sibling_copy(k).start()

    def give_owner(k):
        c = partner(k)

        @pl.when(c >= own_floor)
        def _():
            sibling_copy(k).wait_recv()
            total = dq_acc[c, core] + sib_in[k].astype(F32)

            @pl.when(k == 0)
            def _():
                dq_acc[c, core] = total

            @pl.when(k > 0)
            def _():
                own_out[k] = total.astype(BF16)
                owner_copy(k).start()

    def grad_y(s, d):
        return pltpu.make_async_remote_copy(
            src_ref=y_out.at[s, d - 1],
            dst_ref=y_in.at[s, d - 1],
            send_sem=gy_send.at[s, d - 1],
            recv_sem=gy_recv.at[s, d - 1],
            device_id=y_peer(d),
            device_id_type=MESH,
        )

    def grad_z(s, d):
        return pltpu.make_async_remote_copy(
            src_ref=z_out.at[s, :, (zh + d) % 4],
            dst_ref=z_in.at[s, d],
            send_sem=gz_send.at[s, d],
            recv_sem=gz_recv.at[s, d],
            device_id=z_peer(d),
            device_id_type=MESH,
        )

    def give_y(s):
        for d in range(1, 4):
            y_out[s, d - 1] = acc[s, :, pl.ds(4 * ((y + d) % 4), 4)].astype(BF16)
            grad_y(s, d).start()

    def give_z(s):
        for d in range(1, 4):
            grad_y(s, d).wait_recv()
        total = acc[s, :, pl.ds(4 * y, 4)]
        for d in range(1, 4):
            total = total + y_in[s, d - 1].astype(F32)
        z_out[s] = total.astype(BF16)
        for d in range(1, 4):
            grad_z(s, d).start()

        @pl.when(far)
        def _():
            grad_z(s, 0).start()

        @pl.when(jnp.logical_not(far))
        def _():
            z_in[s, 0] = z_out[s, :, zh]

    def take_z(s):
        for d in range(1, 4):
            grad_z(s, d).wait_recv()

        @pl.when(far)
        def _():
            grad_z(s, 0).wait_recv()

        total = z_in[s, 0].astype(F32)
        for d in range(1, 4):
            total = total + z_in[s, d].astype(F32)
        rows = slice(HALF * s, HALF * (s + 1))
        dk_out[rows] = (total[0] * SCALE).astype(BF16)
        dv_out[rows] = total[1].astype(BF16)

    def step(t, carry):
        k = jnp.where(t < 8, t // 2, jnp.where(t < 12, t - 4, t - 8))
        s = jnp.where(t < 8, t % 2, jnp.where(t < 12, 0, 1))
        c = partner(k)
        seen = c >= own_floor
        ahead = jnp.where(t < 8, t // 2 + 1, t - 3)
        look = jnp.where(t < 8, t % 2 == 0, t < 11)

        @pl.when(look & (partner(ahead) >= own_floor))
        def _():
            query_copy(ahead).wait_recv()
            forward_copy(ahead).start()

        @pl.when(t == 1)
        def _():
            for d in range(1, 4):
                key_y(1, d).wait_recv()

        @pl.when(t == 12)
        def _():
            give_y(0)

        @pl.when(t == 14)
        def _():
            give_z(0)

        @pl.when(seen & (s == 0) & (k > 0))
        def _():
            forward_copy(k).wait_recv()

        def by_half(half, carry):
            plane = jnp.where(half == 0, o, 15 - o)
            low = plane // 2

            @pl.when(c > low)
            def _():
                tile(c, (0, 1), s, half, plane, False)

            @pl.when(c == low)
            def _():
                def by_core(u, carry):
                    @pl.when(2 * c + u >= plane)
                    def _():
                        tile(c, (u,), s, half, plane, True)

                    return carry

                lax.fori_loop(0, 2, by_core, 0)

            return carry

        lax.fori_loop(0, 2, by_half, 0)

        @pl.when(s == 1)
        def _():
            give_sibling(k)

            @pl.when(k > 0)
            def _():
                give_owner(k - 1)

        return carry

    lax.fori_loop(0, 16, step, 0)

    give_y(1)
    give_owner(jnp.int32(7))
    give_z(1)
    take_z(0)

    for k in range(1, 8):

        @pl.when(chip >= floor_of(chips[k]))
        def _(k=k):
            owner_copy(k).wait_recv()
            dq_acc[chip, core] += own_in[k].astype(F32)

    for h in range(HEADS):
        rows = slice(ROWS * h, ROWS * (h + 1))
        dq_out[:, WIDTH * h : WIDTH * (h + 1)] = (dq_acc[chip, core, rows] * SCALE).astype(BF16)
    take_z(1)

    forward_copy(0).wait_send()
    sibling_copy(0).wait_send()
    for k in range(1, 8):

        @pl.when(chip >= floor_of(chips[k]))
        def _(k=k):
            query_copy(k).wait_send()

        @pl.when(chips[k] >= own_floor)
        def _(k=k):
            forward_copy(k).wait_send()
            sibling_copy(k).wait_send()
            owner_copy(k).wait_send()

    for s in range(2):
        for d in range(1, 4):
            key_z(s, d).wait_send()
            key_y(s, d).wait_send()
            grad_y(s, d).wait_send()
            grad_z(s, d).wait_send()

        @pl.when(far)
        def _(s=s):
            key_z(s, 0).wait_send()
            grad_z(s, 0).wait_send()


def local(queries, key_rows, value_rows, forward_out, out_grad, log_norm):
    vmem = pl.BlockSpec(memory_space=pltpu.VMEM)
    dma = pltpu.SemaphoreType.DMA
    return pl.pallas_call(
        attention_grads,
        name="attention_grads",
        out_shape=(
            jax.ShapeDtypeStruct(queries.shape, BF16),
            jax.ShapeDtypeStruct(key_rows.shape, BF16),
            jax.ShapeDtypeStruct(value_rows.shape, BF16),
        ),
        in_specs=[vmem] * 6,
        out_specs=(vmem,) * 3,
        scratch_shapes=[
            pltpu.VMEM((8, 2, ROWS, 1152), BF16),
            pltpu.VMEM((2, 2, 16, HALF, 2 * WIDTH), BF16),
            pltpu.VMEM((2, 2, HALF, WIDTH), BF16),
            pltpu.VMEM((2, 2, 16, HALF, WIDTH), F32),
            pltpu.VMEM((8, 2, 512, WIDTH), F32),
            pltpu.VMEM((8, 512, WIDTH), BF16),
            pltpu.VMEM((8, 512, WIDTH), BF16),
            pltpu.VMEM((8, 512, WIDTH), BF16),
            pltpu.VMEM((8, 512, WIDTH), BF16),
            pltpu.VMEM((2, 3, 2, 4, HALF, WIDTH), BF16),
            pltpu.VMEM((2, 3, 2, 4, HALF, WIDTH), BF16),
            pltpu.VMEM((2, 2, 4, HALF, WIDTH), BF16),
            pltpu.VMEM((2, 4, 2, HALF, WIDTH), BF16),
            dma((8,)), dma((8,)), dma((8,)), dma((8,)),
            dma((2, 4)), dma((2, 4)), dma((2, 3)), dma((2, 3)),
            dma((8,)), dma((8,)), dma((8,)), dma((8,)),
            dma((2, 3)), dma((2, 3)), dma((2, 4)), dma((2, 4)),
        ],
        compiler_params=pltpu.CompilerParams(
            collective_id=0, has_side_effects=True, vmem_limit_bytes=56 * 2**20
        ),
    )(queries, key_rows, value_rows, forward_out, out_grad, log_norm)


def solution(mesh):
    placed = P(("outer", "inner"), None)
    return jax.shard_map(
        local,
        mesh=mesh,
        in_specs=(placed,) * 6,
        out_specs=(placed,) * 3,
        check_vma=False,
    )
```

```python
import functools

import jax
import jax.numpy as jnp
import numpy as np
from jax import lax
from jax.experimental import pallas as pl
from jax.experimental.pallas import tpu as pltpu
from jax.sharding import PartitionSpec as P

F32 = jnp.float32
BF16 = jnp.bfloat16
MESH = pl.DeviceIdType.MESH
HEADS = 4
WIDTH = 128
ROWS = 128
HALF = 64
ROOT = float(np.sqrt(128.0))
SCALE = float(1.0 / np.sqrt(128.0))
EXP2_SCALE = float(np.log2(np.e) / np.sqrt(128.0))
NT = (((1,), (1,)), ((), ()))
NN = (((1,), (0,)), ((), ()))
TN = (((0,), (0,)), ((), ()))

dot = functools.partial(lax.dot_general, preferred_element_type=F32)


def attention_grads(
    q_in, k_in, v_in, fo_in, og_in, ln_in,
    dq_out, dk_out, dv_out,
    units, kv, kv_own, acc, dq_acc, sib_out, sib_in, zp_out, zp_in, own_out, own_in,
    y_out, y_in, z_out, z_in,
    q_send, q_recv, x_send, x_recv, f_send, f_recv, kz_send, kz_recv, ky_send, ky_recv,
    s_send, s_recv, p_send, p_recv, o_send, o_recv, gy_send, gy_recv, gz_send, gz_recv,
):
    o = lax.axis_index("outer")
    i = lax.axis_index("inner")
    chip = o // 2
    core = o % 2
    x = o // 4
    zl = chip % 2
    y = i // 4
    zh = i % 4
    sibling = (2 * chip + 1 - core, i)
    pair = (2 * (2 * x + 1 - zl) + core, i)
    far = y >= 2
    z_plane = jnp.where(far, 15 - o, o)
    own_floor = jnp.minimum(chip, 7 - chip)

    def group(j):
        x_one = x + 1 - 2 * (x % 2)
        x_two = jnp.where(x >= 2, x - 2, x + 2)
        return jnp.where(j == 0, x, jnp.where(j == 1, x_one, jnp.where(j == 2, 3 - x, x_two)))

    def meets(j):
        return (group(j) >= 1) | (x == 0) | (x == 3)

    def met_by(j):
        return (x >= 1) | (group(j) == 0) | (group(j) == 3)

    def chip_of(j, zb):
        return 2 * group(j) + jnp.where(zb == 0, zl, 1 - zl)

    def peer(j):
        return (2 * (2 * group(j) + zl) + core, i)

    def z_peer(d):
        return (z_plane, 4 * y + (zh + d) % 4)

    def y_peer(d):
        return (o, 4 * ((y + d) % 4) + zh)

    barrier = pltpu.get_barrier_semaphore()

    def greet(dev):
        pl.semaphore_signal(barrier, inc=1, device_id=dev, device_id_type=MESH)

    for j in range(1, 4):
        greet(peer(j))
    greet(sibling)
    greet(pair)
    for d in range(1, 4):
        greet(z_peer(d))
        greet(y_peer(d))

    @pl.when(far)
    def _():
        greet(z_peer(0))

    kv_own[0] = k_in[...].reshape(2, HALF, WIDTH)
    kv_own[1] = v_in[...].reshape(2, HALF, WIDTH)

    @pl.when(jnp.logical_not(far))
    def _():
        kv[:, :, i] = kv_own[...]

    lane = lax.broadcasted_iota(jnp.int32, (ROWS, WIDTH), 1)
    stat = jnp.zeros((ROWS, WIDTH), F32)
    norms = jnp.concatenate(
        [ln_in[...].astype(F32), jnp.zeros((ROWS - HEADS, ROWS), F32)], axis=0
    ).T
    for h in range(HEADS):
        cols = slice(WIDTH * h, WIDTH * (h + 1))
        shift = norms[:, h : h + 1] * (-ROOT)
        high = shift.astype(BF16).astype(F32)
        rest = shift - high
        mid = rest.astype(BF16).astype(F32)
        low = rest - mid
        delta = jnp.sum(
            og_in[:, cols].astype(F32) * fo_in[:, cols].astype(F32), axis=1, keepdims=True
        ).astype(BF16).astype(F32)
        for at, column in ((4 * h, high), (4 * h + 1, mid), (4 * h + 2, low), (64 + h, -delta)):
            stat = jnp.where(lane == at, column, stat)
    units[chip, core, :, 0:512] = q_in[...]
    units[chip, core, :, 512:1024] = og_in[...]
    units[chip, core, :, 1024:1152] = stat.astype(BF16)

    pl.semaphore_wait(barrier, jnp.where(far, 12, 11))

    def key_z(s, d):
        return pltpu.make_async_remote_copy(
            src_ref=kv_own.at[:, s],
            dst_ref=kv.at[:, s, i],
            send_sem=kz_send.at[s, d],
            recv_sem=kz_recv.at[s, d],
            device_id=z_peer(d),
            device_id_type=MESH,
        )

    def key_y(s, d, e):
        part = kv.at[:, s, 4 * y + (zh + 4 - e) % 4]
        return pltpu.make_async_remote_copy(
            src_ref=part,
            dst_ref=part,
            send_sem=ky_send.at[s, d - 1, e],
            recv_sem=ky_recv.at[s, d - 1, e],
            device_id=y_peer(d),
            device_id_type=MESH,
        )

    def start_key_z(s):
        for d in range(1, 4):
            key_z(s, d).start()

        @pl.when(far)
        def _():
            key_z(s, 0).start()

    def start_key_y(s, e):
        for d in range(1, 4):
            key_y(s, d, e).start()

    def pass_keys(s):
        @pl.when(far)
        def _():
            key_z(s, 0).wait_recv()
            start_key_y(s, 0)

        for e in range(1, 4):
            key_z(s, e).wait_recv()
            start_key_y(s, e)

    def wait_key_y(s):
        for d in range(1, 4):
            for e in range(4):
                key_y(s, d, e).wait_recv()

    def start_keys(s):
        start_key_z(s)

        @pl.when(jnp.logical_not(far))
        def _():
            start_key_y(s, 0)

    start_keys(0)

    def query_copy(j, zb):
        src = units.at[chip_of(0, zb), core]
        return pltpu.make_async_remote_copy(
            src_ref=src,
            dst_ref=src,
            send_sem=q_send.at[j, zb],
            recv_sem=q_recv.at[j, zb],
            device_id=peer(j),
            device_id_type=MESH,
        )

    def pair_copy():
        src = units.at[chip, core]
        return pltpu.make_async_remote_copy(
            src_ref=src,
            dst_ref=src,
            send_sem=q_send.at[0, 1],
            recv_sem=q_recv.at[0, 1],
            device_id=pair,
            device_id_type=MESH,
        )

    def half_copy(j, zb):
        rows = pl.ds(HALF * (j - 1), HALF)
        src = units.at[chip_of(j, zb), core, rows]
        return pltpu.make_async_remote_copy(
            src_ref=src,
            dst_ref=src,
            send_sem=x_send.at[j - 1, zb],
            recv_sem=x_recv.at[j - 1, zb],
            device_id=peer(3 - j),
            device_id_type=MESH,
        )

    def forward_copy(j, zb):
        part = units.at[chip_of(j, zb), core]
        return pltpu.make_async_remote_copy(
            src_ref=part,
            dst_ref=part,
            send_sem=f_send.at[j, zb],
            recv_sem=f_recv.at[j, zb],
            device_id=sibling,
            device_id_type=MESH,
        )

    def give_query(j, zb):
        @pl.when(met_by(j))
        def _():
            query_copy(j, zb).start()

    def take_query(j, zb):
        @pl.when(meets(j))
        def _():
            query_copy(j, zb).wait_recv()

            @pl.when(group(j) >= 1)
            def _():
                half_copy(j, zb).start()

            @pl.when(chip_of(j, zb) >= own_floor)
            def _():
                forward_copy(j, zb).start()

    def take_halves(zb):
        @pl.when(meets(3))
        def _():
            half_copy(1, zb).wait_recv()
            half_copy(2, zb).wait_recv()

            @pl.when(chip_of(3, zb) >= own_floor)
            def _():
                forward_copy(3, zb).start()

    def take_pair():
        pair_copy().wait_recv()
        give_query(1, 1)
        give_query(2, 1)
        forward_copy(0, 1).start()

    give_query(1, 0)
    give_query(2, 0)
    pair_copy().start()
    forward_copy(0, 0).start()
    start_keys(1)
    acc[...] = jnp.zeros_like(acc)
    dq_acc[...] = jnp.zeros_like(dq_acc)
    pass_keys(0)
    take_query(1, 0)
    take_query(2, 0)
    take_pair()
    pass_keys(1)
    wait_key_y(0)

    def unit_rows(c, u, base):
        return jnp.concatenate(
            [units[c, u, :, base + WIDTH * h : base + WIDTH * (h + 1)] for h in range(HEADS)],
            axis=0,
        )

    def unit_stats(c, u, first):
        st = units[c, u, :, 1024:1152]
        ln = lax.broadcasted_iota(jnp.int32, (ROWS, WIDTH), 1)
        if first:
            keep = [ln // 4 == h for h in range(HEADS)]
        else:
            keep = [ln == 64 + h for h in range(HEADS)]
        return jnp.concatenate([jnp.where(m, st, jnp.zeros_like(st)) for m in keep], axis=0)

    def tile(c, cores, k, v, half, masked_from):
        ones = jnp.ones(k.shape, BF16)
        q = jnp.concatenate([unit_rows(c, u, 0) for u in cores], axis=0)
        g = jnp.concatenate([unit_rows(c, u, 512) for u in cores], axis=0)
        q_stat = jnp.concatenate([unit_stats(c, u, True) for u in cores], axis=0)
        g_stat = jnp.concatenate([unit_stats(c, u, False) for u in cores], axis=0)
        scores = dot(
            jnp.concatenate([k, ones], axis=1), jnp.concatenate([q, q_stat], axis=1), NT
        )
        probs = dot(
            jnp.concatenate([v, ones], axis=1), jnp.concatenate([g, g_stat], axis=1), NT
        )
        w = jnp.exp2(scores * EXP2_SCALE)
        if masked_from is not None:
            row = lax.broadcasted_iota(jnp.int32, (16 * HALF, 1), 0)
            col = lax.broadcasted_iota(jnp.int32, (1, HEADS * ROWS), 1)
            spot = (row // HALF) % 8 * ROWS + row // (8 * HALF) * HALF + row % HALF
            key_pos = (masked_from * 16 + 8 * half) * ROWS + spot
            query_pos = ((2 * c + cores[0]) * 16 + i) * ROWS + col % ROWS
            w = jnp.where(key_pos <= query_pos, w, 0.0)
        gs = (w * probs).astype(BF16)
        w = w.astype(BF16)
        dq = dot(gs, k, TN)
        for n, u in enumerate(cores):
            dq_acc[c, u] += dq[512 * n : 512 * (n + 1)]
        return dot(gs, q, NN), dot(w, g, NN)

    def whole_tiles(c, s):
        def by_half(half, carry):
            @pl.when(c > jnp.where(half == 0, chip, 7 - chip))
            def _():
                keys = pl.ds(8 * half, 8)
                k = kv[0, s, keys].reshape(8 * HALF, WIDTH)
                v = kv[1, s, keys].reshape(8 * HALF, WIDTH)
                dk, dv = tile(c, (0, 1), k, v, half, None)
                acc[s, 0, keys] += dk.reshape(8, HALF, WIDTH)
                acc[s, 1, keys] += dv.reshape(8, HALF, WIDTH)

            return carry

        lax.fori_loop(0, 2, by_half, 0)

    def edge_tiles(c, half):
        plane = jnp.where(half == 0, o, 15 - o)

        def by_core(u, carry):
            unit = 2 * c + u

            @pl.when((unit > plane) | ((unit == plane) & ((half == 0) | far)))
            def _():
                keys = pl.ds(8 * half, 8)
                k = kv[0, :, keys].reshape(16 * HALF, WIDTH)
                v = kv[1, :, keys].reshape(16 * HALF, WIDTH)
                dk, dv = tile(c, (u,), k, v, half, plane)
                acc[:, 0, keys] += dk.reshape(2, 8, HALF, WIDTH)
                acc[:, 1, keys] += dv.reshape(2, 8, HALF, WIDTH)

            return carry

        lax.fori_loop(0, 2, by_core, 0)

    def sibling_copy(j):
        return pltpu.make_async_remote_copy(
            src_ref=sib_out.at[j],
            dst_ref=sib_in.at[j],
            send_sem=s_send.at[j],
            recv_sem=s_recv.at[j],
            device_id=sibling,
            device_id_type=MESH,
        )

    def grad_pair_copy(j):
        return pltpu.make_async_remote_copy(
            src_ref=zp_out.at[j],
            dst_ref=zp_in.at[j],
            send_sem=p_send.at[j],
            recv_sem=p_recv.at[j],
            device_id=pair,
            device_id_type=MESH,
        )

    def owner_copy(j):
        return pltpu.make_async_remote_copy(
            src_ref=own_out.at[j],
            dst_ref=own_in.at[j],
            send_sem=o_send.at[j],
            recv_sem=o_recv.at[j],
            device_id=peer(j),
            device_id_type=MESH,
        )

    def give_sibling(j):
        @pl.when(meets(j))
        def _():
            for zb in range(2):
                sib_out[j, zb] = dq_acc[chip_of(j, zb), 1 - core].astype(BF16)
            sibling_copy(j).start()

    def give_pair(j):
        @pl.when(meets(j))
        def _():
            sibling_copy(j).wait_recv()
            zp_out[j] = (dq_acc[chip_of(j, 1), core] + sib_in[j, 1].astype(F32)).astype(BF16)
            grad_pair_copy(j).start()
            dq_acc[chip_of(j, 0), core] += sib_in[j, 0].astype(F32)

    def give_owner(j):
        @pl.when(meets(j))
        def _():
            grad_pair_copy(j).wait_recv()
            own_out[j] = (dq_acc[chip_of(j, 0), core] + zp_in[j].astype(F32)).astype(BF16)
            owner_copy(j).start()

    def grad_y(s, d, e):
        return pltpu.make_async_remote_copy(
            src_ref=y_out.at[s, d - 1, e],
            dst_ref=y_in.at[s, d - 1, e],
            send_sem=gy_send.at[s, d - 1, e],
            recv_sem=gy_recv.at[s, d - 1, e],
            device_id=y_peer(d),
            device_id_type=MESH,
        )

    def grad_z(s, e):
        return pltpu.make_async_remote_copy(
            src_ref=z_out.at[s, e],
            dst_ref=z_in.at[s, e],
            send_sem=gz_send.at[s, e],
            recv_sem=gz_recv.at[s, e],
            device_id=z_peer(e),
            device_id_type=MESH,
        )

    def give_y(s):
        for e in (2, 1, 3, 0):
            for d in range(1, 4):
                unit = 4 * ((y + d) % 4) + (zh + e) % 4
                y_out[s, d - 1, e] = acc[s, :, unit].astype(BF16)
                grad_y(s, d, e).start()

    def give_z(s):
        for e in (2, 1, 3, 0):
            total = acc[s, :, 4 * y + (zh + e) % 4]
            for d in range(1, 4):
                grad_y(s, d, e).wait_recv()
                total = total + y_in[s, d - 1, e].astype(F32)
            z_out[s, e] = total.astype(BF16)
            if e:
                grad_z(s, e).start()

        @pl.when(far)
        def _():
            grad_z(s, 0).start()

        @pl.when(jnp.logical_not(far))
        def _():
            z_in[s, 0] = z_out[s, 0]

    def take_z(s):
        for d in range(1, 4):
            grad_z(s, d).wait_recv()

        @pl.when(far)
        def _():
            grad_z(s, 0).wait_recv()

        total = z_in[s, 0].astype(F32)
        for d in range(1, 4):
            total = total + z_in[s, d].astype(F32)
        rows = slice(HALF * s, HALF * (s + 1))
        dk_out[rows] = (total[0] * SCALE).astype(BF16)
        dv_out[rows] = total[1].astype(BF16)

    steps = (
        (1, 0, 0), (2, 0, 0), (0, 0, 0), (0, 1, 0), (1, 0, 1), (2, 0, 1), (0, 0, 2),
        (1, 1, 0), (1, 1, 1), (2, 1, 0), (2, 1, 2), (3, 0, 0), (3, 1, 0),
        (2, 1, 1), (3, 0, 1), (3, 1, 1), (0, 0, 1), (0, 1, 1),
    )

    def pick(t, column):
        value = jnp.int32(steps[-1][column])
        for n in range(len(steps) - 2, -1, -1):
            value = jnp.where(t == n, steps[n][column], value)
        return value

    def on(cond, call, *args):
        @pl.when(cond)
        def _():
            call(*args)

    def step(t, carry):
        j = pick(t, 0)
        zb = pick(t, 1)
        s = pick(t, 2)
        c = chip_of(j, zb)

        on(t == 4, wait_key_y, 1)
        on(t == 13, give_y, 0)
        on(t == 15, give_z, 0)

        @pl.when((s == 0) & ((j == 0) | (c >= own_floor)))
        def _():
            forward_copy(j, zb).wait_recv()

        @pl.when(s < 2)
        def _():
            whole_tiles(c, s)

        @pl.when(s == 2)
        def _():
            edge_tiles(c, jnp.where(j == 0, 0, 1))

        on(t == 4, take_query, 1, 1)
        on(t == 5, take_query, 2, 1)
        on(t == 5, take_halves, 0)
        on(t == 9, take_halves, 1)
        on(t == 8, give_sibling, 1)
        on(t == 10, give_pair, 1)
        on(t == 12, give_owner, 1)
        on(t == 13, give_sibling, 2)
        on(t == 14, give_pair, 2)
        on(t == 15, give_sibling, 3)
        on(t == 16, give_owner, 2)
        on(t == 16, give_pair, 3)
        return carry

    lax.fori_loop(0, len(steps), step, 0)

    give_y(1)
    give_sibling(0)
    give_owner(3)
    give_pair(0)
    give_z(1)
    take_z(0)

    for j in range(1, 4):

        @pl.when(met_by(j))
        def _(j=j):
            owner_copy(j).wait_recv()
            dq_acc[chip, core] += own_in[j].astype(F32)

    grad_pair_copy(0).wait_recv()
    for h in range(HEADS):
        rows = slice(ROWS * h, ROWS * (h + 1))
        total = dq_acc[chip, core, rows] + zp_in[0, rows].astype(F32)
        dq_out[:, WIDTH * h : WIDTH * (h + 1)] = (total * SCALE).astype(BF16)
    take_z(1)

    pair_copy().wait_send()
    for j in range(4):
        if j:

            @pl.when(met_by(j))
            def _(j=j):
                if j < 3:
                    query_copy(j, 0).wait_send()
                    query_copy(j, 1).wait_send()

        if j in (1, 2):

            @pl.when(group(j) >= 1)
            def _(j=j):
                half_copy(j, 0).wait_send()
                half_copy(j, 1).wait_send()

        @pl.when(meets(j))
        def _(j=j):
            sibling_copy(j).wait_send()
            grad_pair_copy(j).wait_send()
            if j:
                owner_copy(j).wait_send()

        for zb in range(2):

            @pl.when((j == 0) | (chip_of(j, zb) >= own_floor))
            def _(j=j, zb=zb):
                forward_copy(j, zb).wait_send()

    for s in range(2):
        for d in range(1, 4):
            key_z(s, d).wait_send()
            grad_z(s, d).wait_send()
            for e in range(4):
                key_y(s, d, e).wait_send()
                grad_y(s, d, e).wait_send()

        @pl.when(far)
        def _(s=s):
            key_z(s, 0).wait_send()
            grad_z(s, 0).wait_send()


def local(queries, key_rows, value_rows, forward_out, out_grad, log_norm):
    vmem = pl.BlockSpec(memory_space=pltpu.VMEM)
    dma = pltpu.SemaphoreType.DMA
    return pl.pallas_call(
        attention_grads,
        name="attention_grads",
        out_shape=(
            jax.ShapeDtypeStruct(queries.shape, BF16),
            jax.ShapeDtypeStruct(key_rows.shape, BF16),
            jax.ShapeDtypeStruct(value_rows.shape, BF16),
        ),
        in_specs=[vmem] * 6,
        out_specs=(vmem,) * 3,
        scratch_shapes=[
            pltpu.VMEM((8, 2, ROWS, 1152), BF16),
            pltpu.VMEM((2, 2, 16, HALF, WIDTH), BF16),
            pltpu.VMEM((2, 2, HALF, WIDTH), BF16),
            pltpu.VMEM((2, 2, 16, HALF, WIDTH), F32),
            pltpu.VMEM((8, 2, 512, WIDTH), F32),
            pltpu.VMEM((4, 2, 512, WIDTH), BF16),
            pltpu.VMEM((4, 2, 512, WIDTH), BF16),
            pltpu.VMEM((4, 512, WIDTH), BF16),
            pltpu.VMEM((4, 512, WIDTH), BF16),
            pltpu.VMEM((4, 512, WIDTH), BF16),
            pltpu.VMEM((4, 512, WIDTH), BF16),
            pltpu.VMEM((2, 3, 4, 2, HALF, WIDTH), BF16),
            pltpu.VMEM((2, 3, 4, 2, HALF, WIDTH), BF16),
            pltpu.VMEM((2, 4, 2, HALF, WIDTH), BF16),
            pltpu.VMEM((2, 4, 2, HALF, WIDTH), BF16),
            dma((4, 2)), dma((4, 2)), dma((2, 2)), dma((2, 2)), dma((4, 2)), dma((4, 2)),
            dma((2, 4)), dma((2, 4)), dma((2, 3, 4)), dma((2, 3, 4)),
            dma((4,)), dma((4,)), dma((4,)), dma((4,)), dma((4,)), dma((4,)),
            dma((2, 3, 4)), dma((2, 3, 4)), dma((2, 4)), dma((2, 4)),
        ],
        compiler_params=pltpu.CompilerParams(
            collective_id=0, has_side_effects=True, vmem_limit_bytes=56 * 2**20
        ),
    )(queries, key_rows, value_rows, forward_out, out_grad, log_norm.T)


def solution(mesh):
    placed = P(("outer", "inner"), None)
    return jax.shard_map(
        local,
        mesh=mesh,
        in_specs=(placed,) * 6,
        out_specs=(placed,) * 3,
        check_vma=False,
    )
```

```python
import functools

import jax
import jax.numpy as jnp
import numpy as np
from jax import lax
from jax.experimental import pallas as pl
from jax.experimental.pallas import tpu as pltpu
from jax.sharding import PartitionSpec as P

F32 = jnp.float32
BF16 = jnp.bfloat16
MESH = pl.DeviceIdType.MESH
HEADS = 4
WIDTH = 128
ROWS = 128
HALF = 64
SCALE = float(1.0 / np.sqrt(128.0))
LOG2_E = float(np.log2(np.e))
EXP2_SCALE = float(np.log2(np.e) / np.sqrt(128.0))
SPAN = HEADS * ROWS
UNIT = 2 * SPAN + 16
NT = (((1,), (1,)), ((), ()))
NN = (((1,), (0,)), ((), ()))
TN = (((0,), (0,)), ((), ()))

dot = functools.partial(lax.dot_general, preferred_element_type=F32)


def attention_grads(
    q_in, k_in, v_in, fo_in, og_in, ln_in,
    out,
    units, kv, kv_own, acc, dq_acc, sib_out, sib_in, zp_out, zp_in, own_out, own_in,
    y_out, y_in, z_out, z_in,
    q_send, q_recv, x_send, x_recv, f_send, f_recv, kz_send, kz_recv, ky_send, ky_recv,
    s_send, s_recv, p_send, p_recv, o_send, o_recv, gy_send, gy_recv, gz_send, gz_recv,
):
    o = lax.axis_index("outer")
    i = lax.axis_index("inner")
    chip = o // 2
    core = o % 2
    x = o // 4
    zl = chip % 2
    y = i // 4
    zh = i % 4
    sibling = (2 * chip + 1 - core, i)
    pair = (2 * (2 * x + 1 - zl) + core, i)
    far = y >= 2
    z_plane = jnp.where(far, 15 - o, o)
    own_floor = jnp.minimum(chip, 7 - chip)

    def group(j):
        x_one = x + 1 - 2 * (x % 2)
        x_two = jnp.where(x >= 2, x - 2, x + 2)
        return jnp.where(j == 0, x, jnp.where(j == 1, x_one, jnp.where(j == 2, 3 - x, x_two)))

    def meets(j):
        return (group(j) >= 1) | (x == 0) | (x == 3)

    def met_by(j):
        return (x >= 1) | (group(j) == 0) | (group(j) == 3)

    def chip_of(j, zb):
        return 2 * group(j) + jnp.where(zb == 0, zl, 1 - zl)

    def peer(j):
        return (2 * (2 * group(j) + zl) + core, i)

    def z_peer(d):
        return (z_plane, 4 * y + (zh + d) % 4)

    def y_peer(d):
        return (o, 4 * ((y + d) % 4) + zh)

    barrier = pltpu.get_barrier_semaphore()

    def greet(dev):
        pl.semaphore_signal(barrier, inc=1, device_id=dev, device_id_type=MESH)

    for j in range(1, 4):
        greet(peer(j))
    greet(sibling)
    greet(pair)
    for d in range(1, 4):
        greet(z_peer(d))
        greet(y_peer(d))

    @pl.when(far)
    def _():
        greet(z_peer(0))

    kv_own[0] = k_in[...].reshape(2, HALF, WIDTH)
    kv_own[1] = v_in[...].reshape(2, HALF, WIDTH)

    @pl.when(jnp.logical_not(far))
    def _():
        kv[:, :, i] = kv_own[...]

    pl.semaphore_wait(barrier, jnp.where(far, 12, 11))

    def key_z(s, d):
        return pltpu.make_async_remote_copy(
            src_ref=kv_own.at[:, s],
            dst_ref=kv.at[:, s, i],
            send_sem=kz_send.at[s, d],
            recv_sem=kz_recv.at[s, d],
            device_id=z_peer(d),
            device_id_type=MESH,
        )

    def key_y(s, d, e):
        part = kv.at[:, s, 4 * y + (zh + 4 - e) % 4]
        return pltpu.make_async_remote_copy(
            src_ref=part,
            dst_ref=part,
            send_sem=ky_send.at[s, d - 1, e],
            recv_sem=ky_recv.at[s, d - 1, e],
            device_id=y_peer(d),
            device_id_type=MESH,
        )

    def start_key_z(s):
        for d in range(1, 4):
            key_z(s, d).start()

        @pl.when(far)
        def _():
            key_z(s, 0).start()

    def start_key_y(s, e):
        for d in range(1, 4):
            key_y(s, d, e).start()

    def pass_keys(s):
        @pl.when(far)
        def _():
            key_z(s, 0).wait_recv()
            start_key_y(s, 0)

        for e in range(1, 4):
            key_z(s, e).wait_recv()
            start_key_y(s, e)

    def wait_key_y(s):
        for d in range(1, 4):
            for e in range(4):
                key_y(s, d, e).wait_recv()

    def start_keys(s):
        start_key_z(s)

        @pl.when(jnp.logical_not(far))
        def _():
            start_key_y(s, 0)

    start_keys(0)

    lane = lax.broadcasted_iota(jnp.int32, (ROWS, WIDTH), 1)
    deltas = jnp.zeros((ROWS, WIDTH), F32)
    for h in range(HEADS):
        cols = slice(WIDTH * h, WIDTH * (h + 1))
        units[chip, core, ROWS * h : ROWS * (h + 1)] = q_in[:, cols]
        units[chip, core, SPAN + ROWS * h : SPAN + ROWS * (h + 1)] = og_in[:, cols]
        delta = jnp.sum(
            og_in[:, cols].astype(F32) * fo_in[:, cols].astype(F32), axis=1, keepdims=True
        )
        deltas = jnp.where(lane == HEADS + h, delta, deltas)
    norms = jnp.concatenate(
        [ln_in[...].astype(F32), jnp.zeros((16 - HEADS, ROWS), F32)], axis=0
    )
    units[chip, core, 2 * SPAN : UNIT] = (norms + deltas.T[0:16]).astype(BF16)

    def query_copy(j, zb):
        src = units.at[chip_of(0, zb), core]
        return pltpu.make_async_remote_copy(
            src_ref=src,
            dst_ref=src,
            send_sem=q_send.at[j, zb],
            recv_sem=q_recv.at[j, zb],
            device_id=peer(j),
            device_id_type=MESH,
        )

    def pair_copy():
        src = units.at[chip, core]
        return pltpu.make_async_remote_copy(
            src_ref=src,
            dst_ref=src,
            send_sem=q_send.at[0, 1],
            recv_sem=q_recv.at[0, 1],
            device_id=pair,
            device_id_type=MESH,
        )

    def half_copy(j, zb):
        rows = pl.ds(0, SPAN) if j == 1 else pl.ds(SPAN, UNIT - SPAN)
        src = units.at[chip_of(j, zb), core, rows]
        return pltpu.make_async_remote_copy(
            src_ref=src,
            dst_ref=src,
            send_sem=x_send.at[j - 1, zb],
            recv_sem=x_recv.at[j - 1, zb],
            device_id=peer(3 - j),
            device_id_type=MESH,
        )

    def forward_copy(j, zb):
        part = units.at[chip_of(j, zb), core]
        return pltpu.make_async_remote_copy(
            src_ref=part,
            dst_ref=part,
            send_sem=f_send.at[j, zb],
            recv_sem=f_recv.at[j, zb],
            device_id=sibling,
            device_id_type=MESH,
        )

    def give_query(j, zb):
        @pl.when(met_by(j))
        def _():
            query_copy(j, zb).start()

    def take_query(j, zb):
        @pl.when(meets(j))
        def _():
            query_copy(j, zb).wait_recv()

            @pl.when(group(j) >= 1)
            def _():
                half_copy(j, zb).start()

            @pl.when(chip_of(j, zb) >= own_floor)
            def _():
                forward_copy(j, zb).start()

    def take_halves(zb):
        @pl.when(meets(3))
        def _():
            half_copy(1, zb).wait_recv()
            half_copy(2, zb).wait_recv()

            @pl.when(chip_of(3, zb) >= own_floor)
            def _():
                forward_copy(3, zb).start()

    def take_pair():
        pair_copy().wait_recv()
        give_query(1, 1)
        give_query(2, 1)
        forward_copy(0, 1).start()

    give_query(1, 0)
    give_query(2, 0)
    pair_copy().start()
    forward_copy(0, 0).start()
    start_keys(1)
    acc[...] = jnp.zeros_like(acc)
    dq_acc[...] = jnp.zeros_like(dq_acc)
    pass_keys(0)
    take_query(1, 0)
    take_query(2, 0)
    take_pair()
    pass_keys(1)
    wait_key_y(0)

    def unit_rows(c, cores, base):
        return jnp.concatenate([units[c, u, base : base + SPAN] for u in cores], axis=0)

    def unit_row(c, cores, first):
        stats = [units[c, u, 2 * SPAN : UNIT].astype(F32) for u in cores]
        return jnp.concatenate(
            [st[first + h : first + h + 1] for st in stats for h in range(HEADS)], axis=1
        )

    def tile(c, cores, k, v, half, masked_from):
        q = unit_rows(c, cores, 0)
        g = unit_rows(c, cores, SPAN)
        norm = unit_row(c, cores, 0) * LOG2_E
        delta = unit_row(c, cores, HEADS)
        scores = dot(k, q, NT)
        probs = dot(v, g, NT)
        w = jnp.exp2(scores * EXP2_SCALE - norm)
        if masked_from is not None:
            row = lax.broadcasted_iota(jnp.int32, (16 * HALF, 1), 0)
            col = lax.broadcasted_iota(jnp.int32, (1, HEADS * ROWS), 1)
            spot = (row // HALF) % 8 * ROWS + row // (8 * HALF) * HALF + row % HALF
            key_pos = (masked_from * 16 + 8 * half) * ROWS + spot
            query_pos = ((2 * c + cores[0]) * 16 + i) * ROWS + col % ROWS
            w = jnp.where(key_pos <= query_pos, w, 0.0)
        gs = (w * (probs - delta)).astype(BF16)
        w = w.astype(BF16)
        dq = dot(gs, k, TN)
        for n, u in enumerate(cores):
            dq_acc[c, u] += dq[512 * n : 512 * (n + 1)]
        return dot(gs, q, NN), dot(w, g, NN)

    def whole_tiles(c, s):
        def by_half(half, carry):
            @pl.when(c > jnp.where(half == 0, chip, 7 - chip))
            def _():
                keys = pl.ds(8 * half, 8)
                k = kv[0, s, keys].reshape(8 * HALF, WIDTH)
                v = kv[1, s, keys].reshape(8 * HALF, WIDTH)
                dk, dv = tile(c, (0, 1), k, v, half, None)
                acc[s, 0, keys] += dk.reshape(8, HALF, WIDTH)
                acc[s, 1, keys] += dv.reshape(8, HALF, WIDTH)

            return carry

        lax.fori_loop(0, 2, by_half, 0)

    def edge_tiles(c, half):
        plane = jnp.where(half == 0, o, 15 - o)

        def by_core(u, carry):
            unit = 2 * c + u

            @pl.when((unit > plane) | ((unit == plane) & ((half == 0) | far)))
            def _():
                keys = pl.ds(8 * half, 8)
                k = kv[0, :, keys].reshape(16 * HALF, WIDTH)
                v = kv[1, :, keys].reshape(16 * HALF, WIDTH)
                dk, dv = tile(c, (u,), k, v, half, plane)
                acc[:, 0, keys] += dk.reshape(2, 8, HALF, WIDTH)
                acc[:, 1, keys] += dv.reshape(2, 8, HALF, WIDTH)

            return carry

        lax.fori_loop(0, 2, by_core, 0)

    def sibling_copy(j):
        return pltpu.make_async_remote_copy(
            src_ref=sib_out.at[j],
            dst_ref=sib_in.at[j],
            send_sem=s_send.at[j],
            recv_sem=s_recv.at[j],
            device_id=sibling,
            device_id_type=MESH,
        )

    def grad_pair_copy(j):
        return pltpu.make_async_remote_copy(
            src_ref=zp_out.at[j],
            dst_ref=zp_in.at[j],
            send_sem=p_send.at[j],
            recv_sem=p_recv.at[j],
            device_id=pair,
            device_id_type=MESH,
        )

    def owner_copy(j):
        return pltpu.make_async_remote_copy(
            src_ref=own_out.at[j],
            dst_ref=own_in.at[j],
            send_sem=o_send.at[j],
            recv_sem=o_recv.at[j],
            device_id=peer(j),
            device_id_type=MESH,
        )

    def give_sibling(j):
        @pl.when(meets(j))
        def _():
            for zb in range(2):
                sib_out[j, zb] = dq_acc[chip_of(j, zb), 1 - core].astype(BF16)
            sibling_copy(j).start()

    def give_pair(j):
        @pl.when(meets(j))
        def _():
            sibling_copy(j).wait_recv()
            zp_out[j] = (dq_acc[chip_of(j, 1), core] + sib_in[j, 1].astype(F32)).astype(BF16)
            grad_pair_copy(j).start()
            dq_acc[chip_of(j, 0), core] += sib_in[j, 0].astype(F32)

    def give_owner(j):
        @pl.when(meets(j))
        def _():
            grad_pair_copy(j).wait_recv()
            own_out[j] = (dq_acc[chip_of(j, 0), core] + zp_in[j].astype(F32)).astype(BF16)
            owner_copy(j).start()

    def grad_y(s, d, e):
        return pltpu.make_async_remote_copy(
            src_ref=y_out.at[s, d - 1, e],
            dst_ref=y_in.at[s, d - 1, e],
            send_sem=gy_send.at[s, d - 1, e],
            recv_sem=gy_recv.at[s, d - 1, e],
            device_id=y_peer(d),
            device_id_type=MESH,
        )

    def grad_z(s, e):
        return pltpu.make_async_remote_copy(
            src_ref=z_out.at[s, e],
            dst_ref=z_in.at[s, e],
            send_sem=gz_send.at[s, e],
            recv_sem=gz_recv.at[s, e],
            device_id=z_peer(e),
            device_id_type=MESH,
        )

    def give_y(s):
        for e in (2, 1, 3, 0):
            for d in range(1, 4):
                unit = 4 * ((y + d) % 4) + (zh + e) % 4
                y_out[s, d - 1, e] = acc[s, :, unit].astype(BF16)
                grad_y(s, d, e).start()

    def give_z(s, order=(2, 1, 3, 0)):
        for e in order:
            total = acc[s, :, 4 * y + (zh + e) % 4]
            for d in range(1, 4):
                grad_y(s, d, e).wait_recv()
                total = total + y_in[s, d - 1, e].astype(F32)
            z_out[s, e] = total.astype(BF16)
            if e:
                grad_z(s, e).start()
        if 0 not in order:
            return

        @pl.when(far)
        def _():
            grad_z(s, 0).start()

        @pl.when(jnp.logical_not(far))
        def _():
            z_in[s, 0] = z_out[s, 0]

    def take_z(s):
        for d in range(1, 4):
            grad_z(s, d).wait_recv()

        @pl.when(far)
        def _():
            grad_z(s, 0).wait_recv()

        total = z_in[s, 0].astype(F32)
        for d in range(1, 4):
            total = total + z_in[s, d].astype(F32)
        rows = slice(HALF * s, HALF * (s + 1))
        out[rows, 4 * WIDTH : 5 * WIDTH] = (total[0] * SCALE).astype(BF16)
        out[rows, 5 * WIDTH :] = total[1].astype(BF16)

    steps = (
        (1, 0, 0),
        (2, 0, 0),
        (0, 0, 0),
        (0, 1, 0),
        (1, 0, 1),
        (2, 0, 1),
        (0, 0, 2),
        (1, 1, 0),
        (2, 1, 0),
        (2, 1, 2),
        (3, 0, 0),
        (3, 1, 0),
        (1, 1, 1),
        (2, 1, 1),
        (3, 0, 1),
        (3, 1, 1),
        (0, 0, 1),
        (0, 1, 1),
    )

    def pick(t, column):
        value = jnp.int32(steps[-1][column])
        for n in range(len(steps) - 2, -1, -1):
            value = jnp.where(t == n, steps[n][column], value)
        return value

    def on(cond, call, *args):
        @pl.when(cond)
        def _():
            call(*args)

    def step(t, carry):
        j = pick(t, 0)
        zb = pick(t, 1)
        s = pick(t, 2)
        c = chip_of(j, zb)

        on(t == 4, wait_key_y, 1)
        on(t == 12, give_y, 0)
        on(t == 16, give_z, 0)

        @pl.when((s == 0) & ((j == 0) | (c >= own_floor)))
        def _():
            forward_copy(j, zb).wait_recv()

        @pl.when(s < 2)
        def _():
            whole_tiles(c, s)

        @pl.when(s == 2)
        def _():
            edge_tiles(c, jnp.where(j == 0, 0, 1))

        on(t == 3, take_query, 1, 1)
        on(t == 4, take_query, 2, 1)
        on(t == 4, take_halves, 0)
        on(t == 8, take_halves, 1)
        on(t == 12, give_sibling, 1)
        on(t == 13, give_sibling, 2)
        on(t == 14, give_pair, 1)
        on(t == 15, give_pair, 2)
        on(t == 15, give_sibling, 3)
        on(t == 16, give_owner, 1)
        on(t == 17, give_owner, 2)
        on(t == 17, give_pair, 3)
        on(t == 17, give_sibling, 0)
        return carry

    lax.fori_loop(0, len(steps), step, 0)

    give_y(1)
    give_owner(3)
    give_z(1, (2, 1))
    give_pair(0)
    give_z(1, (3, 0))
    take_z(0)

    for j in range(1, 4):

        @pl.when(met_by(j))
        def _(j=j):
            owner_copy(j).wait_recv()
            dq_acc[chip, core] += own_in[j].astype(F32)

    grad_pair_copy(0).wait_recv()
    for h in range(HEADS):
        rows = slice(ROWS * h, ROWS * (h + 1))
        total = dq_acc[chip, core, rows] + zp_in[0, rows].astype(F32)
        out[:, WIDTH * h : WIDTH * (h + 1)] = (total * SCALE).astype(BF16)
    take_z(1)

    pair_copy().wait_send()
    for j in range(4):
        if j:

            @pl.when(met_by(j))
            def _(j=j):
                if j < 3:
                    query_copy(j, 0).wait_send()
                    query_copy(j, 1).wait_send()

        if j in (1, 2):

            @pl.when(group(j) >= 1)
            def _(j=j):
                half_copy(j, 0).wait_send()
                half_copy(j, 1).wait_send()

        @pl.when(meets(j))
        def _(j=j):
            sibling_copy(j).wait_send()
            grad_pair_copy(j).wait_send()
            if j:
                owner_copy(j).wait_send()

        for zb in range(2):

            @pl.when((j == 0) | (chip_of(j, zb) >= own_floor))
            def _(j=j, zb=zb):
                forward_copy(j, zb).wait_send()

    for s in range(2):
        for d in range(1, 4):
            key_z(s, d).wait_send()
            grad_z(s, d).wait_send()
            for e in range(4):
                key_y(s, d, e).wait_send()
                grad_y(s, d, e).wait_send()

        @pl.when(far)
        def _(s=s):
            key_z(s, 0).wait_send()
            grad_z(s, 0).wait_send()


def part(whole, dq, dk, dv):
    dq[...] = whole[:, 0 : 4 * WIDTH]
    dk[...] = whole[:, 4 * WIDTH : 5 * WIDTH]
    dv[...] = whole[:, 5 * WIDTH :]


def local(queries, key_rows, value_rows, forward_out, out_grad, log_norm):
    vmem = pl.BlockSpec(memory_space=pltpu.VMEM)
    dma = pltpu.SemaphoreType.DMA
    whole = pl.pallas_call(
        attention_grads,
        name="attention_grads",
        out_shape=jax.ShapeDtypeStruct((ROWS, 6 * WIDTH), BF16),
        in_specs=[vmem] * 6,
        out_specs=vmem,
        scratch_shapes=[
            pltpu.VMEM((8, 2, UNIT, WIDTH), BF16),
            pltpu.VMEM((2, 2, 16, HALF, WIDTH), BF16),
            pltpu.VMEM((2, 2, HALF, WIDTH), BF16),
            pltpu.VMEM((2, 2, 16, HALF, WIDTH), F32),
            pltpu.VMEM((8, 2, 512, WIDTH), F32),
            pltpu.VMEM((4, 2, 512, WIDTH), BF16),
            pltpu.VMEM((4, 2, 512, WIDTH), BF16),
            pltpu.VMEM((4, 512, WIDTH), BF16),
            pltpu.VMEM((4, 512, WIDTH), BF16),
            pltpu.VMEM((4, 512, WIDTH), BF16),
            pltpu.VMEM((4, 512, WIDTH), BF16),
            pltpu.VMEM((2, 3, 4, 2, HALF, WIDTH), BF16),
            pltpu.VMEM((2, 3, 4, 2, HALF, WIDTH), BF16),
            pltpu.VMEM((2, 4, 2, HALF, WIDTH), BF16),
            pltpu.VMEM((2, 4, 2, HALF, WIDTH), BF16),
            dma((4, 2)), dma((4, 2)), dma((2, 2)), dma((2, 2)), dma((4, 2)), dma((4, 2)),
            dma((2, 4)), dma((2, 4)), dma((2, 3, 4)), dma((2, 3, 4)),
            dma((4,)), dma((4,)), dma((4,)), dma((4,)), dma((4,)), dma((4,)),
            dma((2, 3, 4)), dma((2, 3, 4)), dma((2, 4)), dma((2, 4)),
        ],
        compiler_params=pltpu.CompilerParams(
            collective_id=0, has_side_effects=True, vmem_limit_bytes=56 * 2**20
        ),
    )(queries, key_rows, value_rows, forward_out, out_grad, log_norm.T)
    return pl.pallas_call(
        part,
        name="part",
        out_shape=(
            jax.ShapeDtypeStruct(queries.shape, BF16),
            jax.ShapeDtypeStruct(key_rows.shape, BF16),
            jax.ShapeDtypeStruct(value_rows.shape, BF16),
        ),
        in_specs=[vmem],
        out_specs=(vmem,) * 3,
    )(whole)


def solution(mesh):
    placed = P(("outer", "inner"), None)
    return jax.shard_map(
        local,
        mesh=mesh,
        in_specs=(placed,) * 6,
        out_specs=(placed,) * 3,
        check_vma=False,
    )
```

```python
import functools

import jax
import jax.numpy as jnp
import numpy as np
from jax import lax
from jax.experimental import pallas as pl
from jax.experimental.pallas import tpu as pltpu
from jax.sharding import PartitionSpec as P

F32 = jnp.float32
BF16 = jnp.bfloat16
MESH = pl.DeviceIdType.MESH
HEADS = 4
WIDTH = 128
ROWS = 128
HALF = 64
SCALE = float(1.0 / np.sqrt(128.0))
LOG2_E = float(np.log2(np.e))
EXP2_SCALE = float(np.log2(np.e) / np.sqrt(128.0))
SPAN = HEADS * ROWS
UNIT = 2 * SPAN + 16
NT = (((1,), (1,)), ((), ()))
NN = (((1,), (0,)), ((), ()))
TN = (((0,), (0,)), ((), ()))

dot = functools.partial(lax.dot_general, preferred_element_type=F32)


def attention_grads(
    q_in, k_in, v_in, fo_in, og_in, ln_in,
    out,
    units, kv, kv_own, acc, dq_acc, sib_out, sib_in, zp_out, zp_in, own_out, own_in,
    y_out, y_in, z_out, z_in,
    q_send, q_recv, x_send, x_recv, f_send, f_recv, kz_send, kz_recv, ky_send, ky_recv,
    s_send, s_recv, p_send, p_recv, o_send, o_recv, gy_send, gy_recv, gz_send, gz_recv,
):
    o = lax.axis_index("outer")
    i = lax.axis_index("inner")
    chip = o // 2
    core = o % 2
    x = o // 4
    zl = chip % 2
    y = i // 4
    zh = i % 4
    sibling = (2 * chip + 1 - core, i)
    pair = (2 * (2 * x + 1 - zl) + core, i)
    far = y >= 2
    z_plane = jnp.where(far, 15 - o, o)
    own_floor = jnp.minimum(chip, 7 - chip)

    def group(j):
        x_one = x + 1 - 2 * (x % 2)
        x_two = jnp.where(x >= 2, x - 2, x + 2)
        return jnp.where(j == 0, x, jnp.where(j == 1, x_one, jnp.where(j == 2, 3 - x, x_two)))

    def meets(j):
        return (group(j) >= 1) | (x == 0) | (x == 3)

    def met_by(j):
        return (x >= 1) | (group(j) == 0) | (group(j) == 3)

    def chip_of(j, zb):
        return 2 * group(j) + jnp.where(zb == 0, zl, 1 - zl)

    def peer(j):
        return (2 * (2 * group(j) + zl) + core, i)

    def z_peer(d):
        return (z_plane, 4 * y + (zh + d) % 4)

    def y_peer(d):
        return (o, 4 * ((y + d) % 4) + zh)

    barrier = pltpu.get_barrier_semaphore()

    def greet(dev):
        pl.semaphore_signal(barrier, inc=1, device_id=dev, device_id_type=MESH)

    for j in range(1, 4):
        greet(peer(j))
    greet(sibling)
    greet(pair)
    for d in range(1, 4):
        greet(z_peer(d))
        greet(y_peer(d))

    @pl.when(far)
    def _():
        greet(z_peer(0))

    kv_own[0] = k_in[...].reshape(2, HALF, WIDTH)
    kv_own[1] = v_in[...].reshape(2, HALF, WIDTH)

    @pl.when(jnp.logical_not(far))
    def _():
        kv[:, :, i] = kv_own[...]

    pl.semaphore_wait(barrier, jnp.where(far, 12, 11))

    def key_z(s, d):
        return pltpu.make_async_remote_copy(
            src_ref=kv_own.at[:, s],
            dst_ref=kv.at[:, s, i],
            send_sem=kz_send.at[s, d],
            recv_sem=kz_recv.at[s, d],
            device_id=z_peer(d),
            device_id_type=MESH,
        )

    def key_y(s, d, e):
        part = kv.at[:, s, 4 * y + (zh + 4 - e) % 4]
        return pltpu.make_async_remote_copy(
            src_ref=part,
            dst_ref=part,
            send_sem=ky_send.at[s, d - 1, e],
            recv_sem=ky_recv.at[s, d - 1, e],
            device_id=y_peer(d),
            device_id_type=MESH,
        )

    def start_key_z(s):
        for d in range(1, 4):
            key_z(s, d).start()

        @pl.when(far)
        def _():
            key_z(s, 0).start()

    def start_key_y(s, e):
        for d in range(1, 4):
            key_y(s, d, e).start()

    def pass_keys(s):
        @pl.when(far)
        def _():
            key_z(s, 0).wait_recv()
            start_key_y(s, 0)

        for e in range(1, 4):
            key_z(s, e).wait_recv()
            start_key_y(s, e)

    def wait_key_y(s):
        for d in range(1, 4):
            for e in range(4):
                key_y(s, d, e).wait_recv()

    def start_keys(s):
        start_key_z(s)

        @pl.when(jnp.logical_not(far))
        def _():
            start_key_y(s, 0)

    start_keys(0)

    lane = lax.broadcasted_iota(jnp.int32, (ROWS, WIDTH), 1)
    deltas = jnp.zeros((ROWS, WIDTH), F32)
    for h in range(HEADS):
        cols = slice(WIDTH * h, WIDTH * (h + 1))
        units[chip, core, ROWS * h : ROWS * (h + 1)] = q_in[:, cols]
        units[chip, core, SPAN + ROWS * h : SPAN + ROWS * (h + 1)] = og_in[:, cols]
        delta = jnp.sum(
            og_in[:, cols].astype(F32) * fo_in[:, cols].astype(F32), axis=1, keepdims=True
        )
        deltas = jnp.where(lane == HEADS + h, delta, deltas)
    norms = jnp.concatenate(
        [ln_in[...].astype(F32), jnp.zeros((16 - HEADS, ROWS), F32)], axis=0
    )
    units[chip, core, 2 * SPAN : UNIT] = (norms + deltas.T[0:16]).astype(BF16)

    def query_copy(j, zb):
        src = units.at[chip_of(0, zb), core]
        return pltpu.make_async_remote_copy(
            src_ref=src,
            dst_ref=src,
            send_sem=q_send.at[j, zb],
            recv_sem=q_recv.at[j, zb],
            device_id=peer(j),
            device_id_type=MESH,
        )

    def pair_copy():
        src = units.at[chip, core]
        return pltpu.make_async_remote_copy(
            src_ref=src,
            dst_ref=src,
            send_sem=q_send.at[0, 1],
            recv_sem=q_recv.at[0, 1],
            device_id=pair,
            device_id_type=MESH,
        )

    def half_copy(j, zb):
        rows = pl.ds(0, SPAN) if j == 1 else pl.ds(SPAN, UNIT - SPAN)
        src = units.at[chip_of(j, zb), core, rows]
        return pltpu.make_async_remote_copy(
            src_ref=src,
            dst_ref=src,
            send_sem=x_send.at[j - 1, zb],
            recv_sem=x_recv.at[j - 1, zb],
            device_id=peer(3 - j),
            device_id_type=MESH,
        )

    def forward_copy(j, zb):
        part = units.at[chip_of(j, zb), core]
        return pltpu.make_async_remote_copy(
            src_ref=part,
            dst_ref=part,
            send_sem=f_send.at[j, zb],
            recv_sem=f_recv.at[j, zb],
            device_id=sibling,
            device_id_type=MESH,
        )

    def give_query(j, zb):
        @pl.when(met_by(j))
        def _():
            query_copy(j, zb).start()

    def take_query(j, zb):
        @pl.when(meets(j))
        def _():
            query_copy(j, zb).wait_recv()

            @pl.when(group(j) >= 1)
            def _():
                half_copy(j, zb).start()

            @pl.when(chip_of(j, zb) >= own_floor)
            def _():
                forward_copy(j, zb).start()

    def take_halves(zb):
        @pl.when(meets(3))
        def _():
            half_copy(1, zb).wait_recv()
            half_copy(2, zb).wait_recv()

            @pl.when(chip_of(3, zb) >= own_floor)
            def _():
                forward_copy(3, zb).start()

    def take_pair():
        pair_copy().wait_recv()
        give_query(1, 1)
        give_query(2, 1)
        forward_copy(0, 1).start()

    give_query(1, 0)
    give_query(2, 0)
    pair_copy().start()
    forward_copy(0, 0).start()
    start_keys(1)
    acc[...] = jnp.zeros_like(acc)
    dq_acc[...] = jnp.zeros_like(dq_acc)
    pass_keys(0)
    take_query(1, 0)
    take_query(2, 0)
    take_pair()
    pass_keys(1)
    wait_key_y(0)

    def unit_rows(c, cores, base):
        return jnp.concatenate([units[c, u, base : base + SPAN] for u in cores], axis=0)

    def unit_row(c, cores, first):
        stats = [units[c, u, 2 * SPAN : UNIT].astype(F32) for u in cores]
        return jnp.concatenate(
            [st[first + h : first + h + 1] for st in stats for h in range(HEADS)], axis=1
        )

    def tile(c, cores, k, v, half, masked_from):
        q = unit_rows(c, cores, 0)
        g = unit_rows(c, cores, SPAN)
        norm = unit_row(c, cores, 0) * LOG2_E
        delta = unit_row(c, cores, HEADS)
        scores = dot(k, q, NT)
        probs = dot(v, g, NT)
        w = jnp.exp2(scores * EXP2_SCALE - norm)
        if masked_from is not None:
            row = lax.broadcasted_iota(jnp.int32, (16 * HALF, 1), 0)
            col = lax.broadcasted_iota(jnp.int32, (1, HEADS * ROWS), 1)
            spot = (row // HALF) % 8 * ROWS + row // (8 * HALF) * HALF + row % HALF
            key_pos = (masked_from * 16 + 8 * half) * ROWS + spot
            query_pos = ((2 * c + cores[0]) * 16 + i) * ROWS + col % ROWS
            w = jnp.where(key_pos <= query_pos, w, 0.0)
        gs = (w * (probs - delta)).astype(BF16)
        w = w.astype(BF16)
        dq = dot(gs, k, TN)
        for n, u in enumerate(cores):
            dq_acc[c, u] += dq[512 * n : 512 * (n + 1)]
        return dot(gs, q, NN), dot(w, g, NN)

    def whole_tiles(c, s):
        def by_half(half, carry):
            @pl.when(c > jnp.where(half == 0, chip, 7 - chip))
            def _():
                keys = pl.ds(8 * half, 8)
                k = kv[0, s, keys].reshape(8 * HALF, WIDTH)
                v = kv[1, s, keys].reshape(8 * HALF, WIDTH)
                dk, dv = tile(c, (0, 1), k, v, half, None)
                acc[s, 0, keys] += dk.reshape(8, HALF, WIDTH)
                acc[s, 1, keys] += dv.reshape(8, HALF, WIDTH)

            return carry

        lax.fori_loop(0, 2, by_half, 0)

    def edge_tiles(c, half):
        plane = jnp.where(half == 0, o, 15 - o)

        def by_core(u, carry):
            unit = 2 * c + u

            @pl.when((unit > plane) | ((unit == plane) & ((half == 0) | far)))
            def _():
                keys = pl.ds(8 * half, 8)
                k = kv[0, :, keys].reshape(16 * HALF, WIDTH)
                v = kv[1, :, keys].reshape(16 * HALF, WIDTH)
                dk, dv = tile(c, (u,), k, v, half, plane)
                acc[:, 0, keys] += dk.reshape(2, 8, HALF, WIDTH)
                acc[:, 1, keys] += dv.reshape(2, 8, HALF, WIDTH)

            return carry

        lax.fori_loop(0, 2, by_core, 0)

    def sibling_copy(j):
        return pltpu.make_async_remote_copy(
            src_ref=sib_out.at[j],
            dst_ref=sib_in.at[j],
            send_sem=s_send.at[j],
            recv_sem=s_recv.at[j],
            device_id=sibling,
            device_id_type=MESH,
        )

    def grad_pair_copy(j):
        return pltpu.make_async_remote_copy(
            src_ref=zp_out.at[j],
            dst_ref=zp_in.at[j],
            send_sem=p_send.at[j],
            recv_sem=p_recv.at[j],
            device_id=pair,
            device_id_type=MESH,
        )

    def owner_copy(j):
        return pltpu.make_async_remote_copy(
            src_ref=own_out.at[j],
            dst_ref=own_in.at[j],
            send_sem=o_send.at[j],
            recv_sem=o_recv.at[j],
            device_id=peer(j),
            device_id_type=MESH,
        )

    def give_sibling(j):
        @pl.when(meets(j))
        def _():
            for zb in range(2):
                sib_out[j, zb] = dq_acc[chip_of(j, zb), 1 - core].astype(BF16)
            sibling_copy(j).start()

    def give_pair(j):
        @pl.when(meets(j))
        def _():
            sibling_copy(j).wait_recv()
            zp_out[j] = (dq_acc[chip_of(j, 1), core] + sib_in[j, 1].astype(F32)).astype(BF16)
            grad_pair_copy(j).start()
            dq_acc[chip_of(j, 0), core] += sib_in[j, 0].astype(F32)

    def give_owner(j):
        @pl.when(meets(j))
        def _():
            grad_pair_copy(j).wait_recv()
            own_out[j] = (dq_acc[chip_of(j, 0), core] + zp_in[j].astype(F32)).astype(BF16)
            owner_copy(j).start()

    def grad_y(s, d, e):
        return pltpu.make_async_remote_copy(
            src_ref=y_out.at[s, d - 1, e],
            dst_ref=y_in.at[s, d - 1, e],
            send_sem=gy_send.at[s, d - 1, e],
            recv_sem=gy_recv.at[s, d - 1, e],
            device_id=y_peer(d),
            device_id_type=MESH,
        )

    def grad_z(s, e):
        return pltpu.make_async_remote_copy(
            src_ref=z_out.at[s, e],
            dst_ref=z_in.at[s, e],
            send_sem=gz_send.at[s, e],
            recv_sem=gz_recv.at[s, e],
            device_id=z_peer(e),
            device_id_type=MESH,
        )

    def give_y(s):
        for e in (2, 1, 3, 0):
            for d in range(1, 4):
                unit = 4 * ((y + d) % 4) + (zh + e) % 4
                y_out[s, d - 1, e] = acc[s, :, unit].astype(BF16)
                grad_y(s, d, e).start()

    def give_z(s, order=(2, 1, 3, 0)):
        for e in order:
            total = acc[s, :, 4 * y + (zh + e) % 4]
            for d in range(1, 4):
                grad_y(s, d, e).wait_recv()
                total = total + y_in[s, d - 1, e].astype(F32)
            z_out[s, e] = total.astype(BF16)
            if e:
                grad_z(s, e).start()
        if 0 not in order:
            return

        @pl.when(far)
        def _():
            grad_z(s, 0).start()

        @pl.when(jnp.logical_not(far))
        def _():
            z_in[s, 0] = z_out[s, 0]

    def take_z(s):
        for d in range(1, 4):
            grad_z(s, d).wait_recv()

        @pl.when(far)
        def _():
            grad_z(s, 0).wait_recv()

        total = z_in[s, 0].astype(F32)
        for d in range(1, 4):
            total = total + z_in[s, d].astype(F32)
        rows = slice(HALF * s, HALF * (s + 1))
        out[rows, 4 * WIDTH : 5 * WIDTH] = (total[0] * SCALE).astype(BF16)
        out[rows, 5 * WIDTH :] = total[1].astype(BF16)

    steps = (
        (1, 0, 0),
        (2, 0, 0),
        (0, 0, 0),
        (0, 1, 0),
        (1, 0, 1),
        (2, 0, 1),
        (0, 0, 2),
        (3, 0, 0),
        (1, 1, 0),
        (2, 1, 0),
        (2, 1, 2),
        (3, 1, 0),
        (1, 1, 1),
        (2, 1, 1),
        (3, 0, 1),
        (3, 1, 1),
        (0, 0, 1),
        (0, 1, 1),
    )

    def pick(t, column):
        value = jnp.int32(steps[-1][column])
        for n in range(len(steps) - 2, -1, -1):
            value = jnp.where(t == n, steps[n][column], value)
        return value

    def on(cond, call, *args):
        @pl.when(cond)
        def _():
            call(*args)

    def step(t, carry):
        j = pick(t, 0)
        zb = pick(t, 1)
        s = pick(t, 2)
        c = chip_of(j, zb)

        on(t == 4, wait_key_y, 1)
        on(t == 12, give_y, 0)
        on(t == 16, give_z, 0)

        @pl.when((s == 0) & ((j == 0) | (c >= own_floor)))
        def _():
            forward_copy(j, zb).wait_recv()

        @pl.when(s < 2)
        def _():
            whole_tiles(c, s)

        @pl.when(s == 2)
        def _():
            edge_tiles(c, jnp.where(j == 0, 0, 1))

        on(t == 3, take_query, 1, 1)
        on(t == 4, take_query, 2, 1)
        on(t == 3, take_halves, 0)
        on(t == 7, take_halves, 1)
        on(t == 12, give_sibling, 1)
        on(t == 13, give_sibling, 2)
        on(t == 14, give_pair, 1)
        on(t == 15, give_pair, 2)
        on(t == 15, give_sibling, 3)
        on(t == 17, give_owner, 1)
        on(t == 17, give_pair, 3)
        on(t == 17, give_sibling, 0)
        return carry

    lax.fori_loop(0, len(steps), step, 0)

    give_y(1)
    give_owner(2)
    give_z(1, (2, 1))
    give_pair(0)
    give_owner(3)
    give_z(1, (3, 0))
    take_z(0)

    for j in range(1, 4):

        @pl.when(met_by(j))
        def _(j=j):
            owner_copy(j).wait_recv()
            dq_acc[chip, core] += own_in[j].astype(F32)

    grad_pair_copy(0).wait_recv()
    for h in range(HEADS):
        rows = slice(ROWS * h, ROWS * (h + 1))
        total = dq_acc[chip, core, rows] + zp_in[0, rows].astype(F32)
        out[:, WIDTH * h : WIDTH * (h + 1)] = (total * SCALE).astype(BF16)
    take_z(1)

    pair_copy().wait_send()
    for j in range(4):
        if j:

            @pl.when(met_by(j))
            def _(j=j):
                if j < 3:
                    query_copy(j, 0).wait_send()
                    query_copy(j, 1).wait_send()

        if j in (1, 2):

            @pl.when(group(j) >= 1)
            def _(j=j):
                half_copy(j, 0).wait_send()
                half_copy(j, 1).wait_send()

        @pl.when(meets(j))
        def _(j=j):
            sibling_copy(j).wait_send()
            grad_pair_copy(j).wait_send()
            if j:
                owner_copy(j).wait_send()

        for zb in range(2):

            @pl.when((j == 0) | (chip_of(j, zb) >= own_floor))
            def _(j=j, zb=zb):
                forward_copy(j, zb).wait_send()

    for s in range(2):
        for d in range(1, 4):
            key_z(s, d).wait_send()
            grad_z(s, d).wait_send()
            for e in range(4):
                key_y(s, d, e).wait_send()
                grad_y(s, d, e).wait_send()

        @pl.when(far)
        def _(s=s):
            key_z(s, 0).wait_send()
            grad_z(s, 0).wait_send()


def part(whole, dq, dk, dv):
    dq[...] = whole[:, 0 : 4 * WIDTH]
    dk[...] = whole[:, 4 * WIDTH : 5 * WIDTH]
    dv[...] = whole[:, 5 * WIDTH :]


def local(queries, key_rows, value_rows, forward_out, out_grad, log_norm):
    vmem = pl.BlockSpec(memory_space=pltpu.VMEM)
    dma = pltpu.SemaphoreType.DMA
    whole = pl.pallas_call(
        attention_grads,
        name="attention_grads",
        out_shape=jax.ShapeDtypeStruct((ROWS, 6 * WIDTH), BF16),
        in_specs=[vmem] * 6,
        out_specs=vmem,
        scratch_shapes=[
            pltpu.VMEM((8, 2, UNIT, WIDTH), BF16),
            pltpu.VMEM((2, 2, 16, HALF, WIDTH), BF16),
            pltpu.VMEM((2, 2, HALF, WIDTH), BF16),
            pltpu.VMEM((2, 2, 16, HALF, WIDTH), F32),
            pltpu.VMEM((8, 2, 512, WIDTH), F32),
            pltpu.VMEM((4, 2, 512, WIDTH), BF16),
            pltpu.VMEM((4, 2, 512, WIDTH), BF16),
            pltpu.VMEM((4, 512, WIDTH), BF16),
            pltpu.VMEM((4, 512, WIDTH), BF16),
            pltpu.VMEM((4, 512, WIDTH), BF16),
            pltpu.VMEM((4, 512, WIDTH), BF16),
            pltpu.VMEM((2, 3, 4, 2, HALF, WIDTH), BF16),
            pltpu.VMEM((2, 3, 4, 2, HALF, WIDTH), BF16),
            pltpu.VMEM((2, 4, 2, HALF, WIDTH), BF16),
            pltpu.VMEM((2, 4, 2, HALF, WIDTH), BF16),
            dma((4, 2)), dma((4, 2)), dma((2, 2)), dma((2, 2)), dma((4, 2)), dma((4, 2)),
            dma((2, 4)), dma((2, 4)), dma((2, 3, 4)), dma((2, 3, 4)),
            dma((4,)), dma((4,)), dma((4,)), dma((4,)), dma((4,)), dma((4,)),
            dma((2, 3, 4)), dma((2, 3, 4)), dma((2, 4)), dma((2, 4)),
        ],
        compiler_params=pltpu.CompilerParams(
            collective_id=0, has_side_effects=True, vmem_limit_bytes=56 * 2**20
        ),
    )(queries, key_rows, value_rows, forward_out, out_grad, log_norm.T)
    return pl.pallas_call(
        part,
        name="part",
        out_shape=(
            jax.ShapeDtypeStruct(queries.shape, BF16),
            jax.ShapeDtypeStruct(key_rows.shape, BF16),
            jax.ShapeDtypeStruct(value_rows.shape, BF16),
        ),
        in_specs=[vmem],
        out_specs=(vmem,) * 3,
    )(whole)


def solution(mesh):
    placed = P(("outer", "inner"), None)
    return jax.shard_map(
        local,
        mesh=mesh,
        in_specs=(placed,) * 6,
        out_specs=(placed,) * 3,
        check_vma=False,
    )
```

```python
import functools

import jax
import jax.numpy as jnp
import numpy as np
from jax import lax
from jax.experimental import pallas as pl
from jax.experimental.pallas import tpu as pltpu
from jax.sharding import PartitionSpec as P

F32 = jnp.float32
BF16 = jnp.bfloat16
MESH = pl.DeviceIdType.MESH
HEADS = 4
WIDTH = 128
ROWS = 128
HALF = 64
SCALE = float(1.0 / np.sqrt(128.0))
LOG2_E = float(np.log2(np.e))
EXP2_SCALE = float(np.log2(np.e) / np.sqrt(128.0))
SPAN = HEADS * ROWS
UNIT = 2 * SPAN + 16
NT = (((1,), (1,)), ((), ()))
NN = (((1,), (0,)), ((), ()))
TN = (((0,), (0,)), ((), ()))

dot = functools.partial(lax.dot_general, preferred_element_type=F32)


def attention_grads(
    q_in, k_in, v_in, fo_in, og_in, ln_in,
    out,
    units, kv, kv_own, acc, dq_acc, sib_out, sib_in, zp_out, zp_in, own_out, own_in,
    y_out, y_in, z_out, z_in,
    q_send, q_recv, x_send, x_recv, f_send, f_recv, kz_send, kz_recv, ky_send, ky_recv,
    s_send, s_recv, p_send, p_recv, o_send, o_recv, gy_send, gy_recv, gz_send, gz_recv,
):
    o = lax.axis_index("outer")
    i = lax.axis_index("inner")
    chip = o // 2
    core = o % 2
    x = o // 4
    zl = chip % 2
    y = i // 4
    zh = i % 4
    sibling = (2 * chip + 1 - core, i)
    pair = (2 * (2 * x + 1 - zl) + core, i)
    far = y >= 2
    z_plane = jnp.where(far, 15 - o, o)
    own_floor = jnp.minimum(chip, 7 - chip)

    def group(j):
        x_one = x + 1 - 2 * (x % 2)
        x_two = jnp.where(x >= 2, x - 2, x + 2)
        return jnp.where(j == 0, x, jnp.where(j == 1, x_one, jnp.where(j == 2, 3 - x, x_two)))

    def meets(j):
        return (group(j) >= 1) | (x == 0) | (x == 3)

    def met_by(j):
        return (x >= 1) | (group(j) == 0) | (group(j) == 3)

    def chip_of(j, zb):
        return 2 * group(j) + jnp.where(zb == 0, zl, 1 - zl)

    def peer(j):
        return (2 * (2 * group(j) + zl) + core, i)

    def z_peer(d):
        return (z_plane, 4 * y + (zh + d) % 4)

    def y_peer(d):
        return (o, 4 * ((y + d) % 4) + zh)

    barrier = pltpu.get_barrier_semaphore()

    def greet(dev):
        pl.semaphore_signal(barrier, inc=1, device_id=dev, device_id_type=MESH)

    for j in range(1, 4):
        greet(peer(j))
    greet(sibling)
    greet(pair)
    for d in range(1, 4):
        greet(z_peer(d))
        greet(y_peer(d))

    @pl.when(far)
    def _():
        greet(z_peer(0))

    kv_own[0] = k_in[...].reshape(2, HALF, WIDTH)
    kv_own[1] = v_in[...].reshape(2, HALF, WIDTH)

    @pl.when(jnp.logical_not(far))
    def _():
        kv[:, :, i] = kv_own[...]

    pl.semaphore_wait(barrier, jnp.where(far, 12, 11))

    def key_z(s, d):
        return pltpu.make_async_remote_copy(
            src_ref=kv_own.at[:, s],
            dst_ref=kv.at[:, s, i],
            send_sem=kz_send.at[s, d],
            recv_sem=kz_recv.at[s, d],
            device_id=z_peer(d),
            device_id_type=MESH,
        )

    def key_y(s, d, e):
        part = kv.at[:, s, 4 * y + (zh + 4 - e) % 4]
        return pltpu.make_async_remote_copy(
            src_ref=part,
            dst_ref=part,
            send_sem=ky_send.at[s, d - 1, e],
            recv_sem=ky_recv.at[s, d - 1, e],
            device_id=y_peer(d),
            device_id_type=MESH,
        )

    def start_key_z(s):
        for d in (2, 1, 3):
            key_z(s, d).start()

        @pl.when(far)
        def _():
            key_z(s, 0).start()

    def start_key_y(s, e):
        for d in (2, 1, 3):
            key_y(s, d, e).start()

    def pass_keys(s):
        @pl.when(far)
        def _():
            key_z(s, 0).wait_recv()
            start_key_y(s, 0)

        for e in (1, 3, 2):
            key_z(s, e).wait_recv()
            start_key_y(s, e)

    def wait_key_y(s):
        for d in range(1, 4):
            for e in range(4):
                key_y(s, d, e).wait_recv()

    def start_keys(s):
        start_key_z(s)

        @pl.when(jnp.logical_not(far))
        def _():
            start_key_y(s, 0)

    start_keys(0)

    lane = lax.broadcasted_iota(jnp.int32, (ROWS, WIDTH), 1)
    deltas = jnp.zeros((ROWS, WIDTH), F32)
    for h in range(HEADS):
        cols = slice(WIDTH * h, WIDTH * (h + 1))
        units[chip, core, ROWS * h : ROWS * (h + 1)] = q_in[:, cols]
        units[chip, core, SPAN + ROWS * h : SPAN + ROWS * (h + 1)] = og_in[:, cols]
        delta = jnp.sum(
            og_in[:, cols].astype(F32) * fo_in[:, cols].astype(F32), axis=1, keepdims=True
        )
        deltas = jnp.where(lane == HEADS + h, delta, deltas)
    norms = jnp.concatenate(
        [ln_in[...].astype(F32), jnp.zeros((16 - HEADS, ROWS), F32)], axis=0
    )
    units[chip, core, 2 * SPAN : UNIT] = (norms + deltas.T[0:16]).astype(BF16)

    def query_copy(j, zb):
        src = units.at[chip_of(0, zb), core]
        return pltpu.make_async_remote_copy(
            src_ref=src,
            dst_ref=src,
            send_sem=q_send.at[j, zb],
            recv_sem=q_recv.at[j, zb],
            device_id=peer(j),
            device_id_type=MESH,
        )

    def pair_copy():
        src = units.at[chip, core]
        return pltpu.make_async_remote_copy(
            src_ref=src,
            dst_ref=src,
            send_sem=q_send.at[0, 1],
            recv_sem=q_recv.at[0, 1],
            device_id=pair,
            device_id_type=MESH,
        )

    def half_copy(j, zb):
        rows = pl.ds(0, SPAN) if j == 1 else pl.ds(SPAN, UNIT - SPAN)
        src = units.at[chip_of(j, zb), core, rows]
        return pltpu.make_async_remote_copy(
            src_ref=src,
            dst_ref=src,
            send_sem=x_send.at[j - 1, zb],
            recv_sem=x_recv.at[j - 1, zb],
            device_id=peer(3 - j),
            device_id_type=MESH,
        )

    def forward_copy(j, zb):
        part = units.at[chip_of(j, zb), core]
        return pltpu.make_async_remote_copy(
            src_ref=part,
            dst_ref=part,
            send_sem=f_send.at[j, zb],
            recv_sem=f_recv.at[j, zb],
            device_id=sibling,
            device_id_type=MESH,
        )

    def give_query(j, zb):
        @pl.when(met_by(j))
        def _():
            query_copy(j, zb).start()

    def take_query(j, zb):
        @pl.when(meets(j))
        def _():
            query_copy(j, zb).wait_recv()

            @pl.when(group(j) >= 1)
            def _():
                half_copy(j, zb).start()

            @pl.when(chip_of(j, zb) >= own_floor)
            def _():
                forward_copy(j, zb).start()

    def take_halves(zb):
        @pl.when(meets(3))
        def _():
            half_copy(1, zb).wait_recv()
            half_copy(2, zb).wait_recv()

            @pl.when(chip_of(3, zb) >= own_floor)
            def _():
                forward_copy(3, zb).start()

    def take_pair():
        pair_copy().wait_recv()
        give_query(1, 1)
        give_query(2, 1)
        forward_copy(0, 1).start()

    give_query(1, 0)
    give_query(2, 0)
    pair_copy().start()
    forward_copy(0, 0).start()
    start_keys(1)
    acc[...] = jnp.zeros_like(acc)
    dq_acc[...] = jnp.zeros_like(dq_acc)
    pass_keys(0)
    take_query(1, 0)
    take_query(2, 0)
    take_pair()
    pass_keys(1)
    wait_key_y(0)

    def unit_rows(c, cores, base):
        return jnp.concatenate([units[c, u, base : base + SPAN] for u in cores], axis=0)

    def unit_row(c, cores, first):
        stats = [units[c, u, 2 * SPAN : UNIT].astype(F32) for u in cores]
        return jnp.concatenate(
            [st[first + h : first + h + 1] for st in stats for h in range(HEADS)], axis=1
        )

    def tile(c, cores, k, v, half, masked_from):
        q = unit_rows(c, cores, 0)
        g = unit_rows(c, cores, SPAN)
        norm = unit_row(c, cores, 0) * LOG2_E
        delta = unit_row(c, cores, HEADS)
        scores = dot(k, q, NT)
        probs = dot(v, g, NT)
        w = jnp.exp2(scores * EXP2_SCALE - norm)
        if masked_from is not None:
            row = lax.broadcasted_iota(jnp.int32, (16 * HALF, 1), 0)
            col = lax.broadcasted_iota(jnp.int32, (1, HEADS * ROWS), 1)
            spot = (row // HALF) % 8 * ROWS + row // (8 * HALF) * HALF + row % HALF
            key_pos = (masked_from * 16 + 8 * half) * ROWS + spot
            query_pos = ((2 * c + cores[0]) * 16 + i) * ROWS + col % ROWS
            w = jnp.where(key_pos <= query_pos, w, 0.0)
        gs = (w * (probs - delta)).astype(BF16)
        w = w.astype(BF16)
        dq = dot(gs, k, TN)
        for n, u in enumerate(cores):
            dq_acc[c, u] += dq[512 * n : 512 * (n + 1)]
        return dot(gs, q, NN), dot(w, g, NN)

    def whole_tiles(c, s):
        def by_half(half, carry):
            @pl.when(c > jnp.where(half == 0, chip, 7 - chip))
            def _():
                keys = pl.ds(8 * half, 8)
                k = kv[0, s, keys].reshape(8 * HALF, WIDTH)
                v = kv[1, s, keys].reshape(8 * HALF, WIDTH)
                dk, dv = tile(c, (0, 1), k, v, half, None)
                acc[s, 0, keys] += dk.reshape(8, HALF, WIDTH)
                acc[s, 1, keys] += dv.reshape(8, HALF, WIDTH)

            return carry

        lax.fori_loop(0, 2, by_half, 0)

    def edge_tiles(c, half):
        plane = jnp.where(half == 0, o, 15 - o)

        def by_core(u, carry):
            unit = 2 * c + u

            @pl.when((unit > plane) | ((unit == plane) & ((half == 0) | far)))
            def _():
                keys = pl.ds(8 * half, 8)
                k = kv[0, :, keys].reshape(16 * HALF, WIDTH)
                v = kv[1, :, keys].reshape(16 * HALF, WIDTH)
                dk, dv = tile(c, (u,), k, v, half, plane)
                acc[:, 0, keys] += dk.reshape(2, 8, HALF, WIDTH)
                acc[:, 1, keys] += dv.reshape(2, 8, HALF, WIDTH)

            return carry

        lax.fori_loop(0, 2, by_core, 0)

    def sibling_copy(j):
        return pltpu.make_async_remote_copy(
            src_ref=sib_out.at[j],
            dst_ref=sib_in.at[j],
            send_sem=s_send.at[j],
            recv_sem=s_recv.at[j],
            device_id=sibling,
            device_id_type=MESH,
        )

    def grad_pair_copy(j):
        return pltpu.make_async_remote_copy(
            src_ref=zp_out.at[j],
            dst_ref=zp_in.at[j],
            send_sem=p_send.at[j],
            recv_sem=p_recv.at[j],
            device_id=pair,
            device_id_type=MESH,
        )

    def owner_copy(j):
        return pltpu.make_async_remote_copy(
            src_ref=own_out.at[j],
            dst_ref=own_in.at[j],
            send_sem=o_send.at[j],
            recv_sem=o_recv.at[j],
            device_id=peer(j),
            device_id_type=MESH,
        )

    def give_sibling(j):
        @pl.when(meets(j))
        def _():
            for zb in range(2):
                sib_out[j, zb] = dq_acc[chip_of(j, zb), 1 - core].astype(BF16)
            sibling_copy(j).start()

    def give_pair(j):
        @pl.when(meets(j))
        def _():
            sibling_copy(j).wait_recv()
            zp_out[j] = (dq_acc[chip_of(j, 1), core] + sib_in[j, 1].astype(F32)).astype(BF16)
            grad_pair_copy(j).start()
            dq_acc[chip_of(j, 0), core] += sib_in[j, 0].astype(F32)

    def give_owner(j):
        @pl.when(meets(j))
        def _():
            grad_pair_copy(j).wait_recv()
            own_out[j] = (dq_acc[chip_of(j, 0), core] + zp_in[j].astype(F32)).astype(BF16)
            owner_copy(j).start()

    def grad_y(s, d, e):
        return pltpu.make_async_remote_copy(
            src_ref=y_out.at[s, d - 1, e],
            dst_ref=y_in.at[s, d - 1, e],
            send_sem=gy_send.at[s, d - 1, e],
            recv_sem=gy_recv.at[s, d - 1, e],
            device_id=y_peer(d),
            device_id_type=MESH,
        )

    def grad_z(s, e):
        return pltpu.make_async_remote_copy(
            src_ref=z_out.at[s, e],
            dst_ref=z_in.at[s, e],
            send_sem=gz_send.at[s, e],
            recv_sem=gz_recv.at[s, e],
            device_id=z_peer(e),
            device_id_type=MESH,
        )

    def give_y(s):
        for e in (2, 1, 3, 0):
            for d in (2, 1, 3):
                unit = 4 * ((y + d) % 4) + (zh + e) % 4
                y_out[s, d - 1, e] = acc[s, :, unit].astype(BF16)
                grad_y(s, d, e).start()

    def give_z(s, order=(2, 1, 3, 0)):
        for e in order:
            total = acc[s, :, 4 * y + (zh + e) % 4]
            for d in range(1, 4):
                grad_y(s, d, e).wait_recv()
                total = total + y_in[s, d - 1, e].astype(F32)
            z_out[s, e] = total.astype(BF16)
            if e:
                grad_z(s, e).start()
        if 0 not in order:
            return

        @pl.when(far)
        def _():
            grad_z(s, 0).start()

        @pl.when(jnp.logical_not(far))
        def _():
            z_in[s, 0] = z_out[s, 0]

    def take_z(s):
        for d in range(1, 4):
            grad_z(s, d).wait_recv()

        @pl.when(far)
        def _():
            grad_z(s, 0).wait_recv()

        total = z_in[s, 0].astype(F32)
        for d in range(1, 4):
            total = total + z_in[s, d].astype(F32)
        rows = slice(HALF * s, HALF * (s + 1))
        out[rows, 4 * WIDTH : 5 * WIDTH] = (total[0] * SCALE).astype(BF16)
        out[rows, 5 * WIDTH :] = total[1].astype(BF16)

    steps = (
        (1, 0, 0),
        (2, 0, 0),
        (0, 0, 0),
        (0, 1, 0),
        (1, 0, 1),
        (2, 0, 1),
        (0, 0, 2),
        (3, 0, 0),
        (1, 1, 0),
        (2, 1, 0),
        (2, 1, 2),
        (3, 1, 0),
        (1, 1, 1),
        (2, 1, 1),
        (3, 0, 1),
        (3, 1, 1),
        (0, 0, 1),
        (0, 1, 1),
    )

    def pick(t, column):
        value = jnp.int32(steps[-1][column])
        for n in range(len(steps) - 2, -1, -1):
            value = jnp.where(t == n, steps[n][column], value)
        return value

    def on(cond, call, *args):
        @pl.when(cond)
        def _():
            call(*args)

    def step(t, carry):
        j = pick(t, 0)
        zb = pick(t, 1)
        s = pick(t, 2)
        c = chip_of(j, zb)

        on(t == 4, wait_key_y, 1)
        on(t == 12, give_y, 0)
        on(t == 16, give_z, 0)

        @pl.when((s == 0) & ((j == 0) | (c >= own_floor)))
        def _():
            forward_copy(j, zb).wait_recv()

        @pl.when(s < 2)
        def _():
            whole_tiles(c, s)

        @pl.when(s == 2)
        def _():
            edge_tiles(c, jnp.where(j == 0, 0, 1))

        on(t == 3, take_query, 1, 1)
        on(t == 4, take_query, 2, 1)
        on(t == 3, take_halves, 0)
        on(t == 7, take_halves, 1)
        on(t == 12, give_sibling, 1)
        on(t == 13, give_sibling, 2)
        on(t == 14, give_pair, 1)
        on(t == 15, give_pair, 2)
        on(t == 15, give_sibling, 3)
        on(t == 17, give_owner, 1)
        on(t == 17, give_pair, 3)
        on(t == 17, give_sibling, 0)
        return carry

    lax.fori_loop(0, len(steps), step, 0)

    give_y(1)
    give_owner(2)
    give_z(1, (2, 1))
    give_pair(0)
    give_owner(3)
    give_z(1, (3, 0))
    take_z(0)

    for j in range(1, 4):

        @pl.when(met_by(j))
        def _(j=j):
            owner_copy(j).wait_recv()
            dq_acc[chip, core] += own_in[j].astype(F32)

    grad_pair_copy(0).wait_recv()
    for h in range(HEADS):
        rows = slice(ROWS * h, ROWS * (h + 1))
        total = dq_acc[chip, core, rows] + zp_in[0, rows].astype(F32)
        out[:, WIDTH * h : WIDTH * (h + 1)] = (total * SCALE).astype(BF16)
    take_z(1)

    pair_copy().wait_send()
    for j in range(4):
        if j:

            @pl.when(met_by(j))
            def _(j=j):
                if j < 3:
                    query_copy(j, 0).wait_send()
                    query_copy(j, 1).wait_send()

        if j in (1, 2):

            @pl.when(group(j) >= 1)
            def _(j=j):
                half_copy(j, 0).wait_send()
                half_copy(j, 1).wait_send()

        @pl.when(meets(j))
        def _(j=j):
            sibling_copy(j).wait_send()
            grad_pair_copy(j).wait_send()
            if j:
                owner_copy(j).wait_send()

        for zb in range(2):

            @pl.when((j == 0) | (chip_of(j, zb) >= own_floor))
            def _(j=j, zb=zb):
                forward_copy(j, zb).wait_send()

    for s in range(2):
        for d in range(1, 4):
            key_z(s, d).wait_send()
            grad_z(s, d).wait_send()
            for e in range(4):
                key_y(s, d, e).wait_send()
                grad_y(s, d, e).wait_send()

        @pl.when(far)
        def _(s=s):
            key_z(s, 0).wait_send()
            grad_z(s, 0).wait_send()


def part(whole, dq, dk, dv):
    dq[...] = whole[:, 0 : 4 * WIDTH]
    dk[...] = whole[:, 4 * WIDTH : 5 * WIDTH]
    dv[...] = whole[:, 5 * WIDTH :]


def local(queries, key_rows, value_rows, forward_out, out_grad, log_norm):
    vmem = pl.BlockSpec(memory_space=pltpu.VMEM)
    dma = pltpu.SemaphoreType.DMA
    whole = pl.pallas_call(
        attention_grads,
        name="attention_grads",
        out_shape=jax.ShapeDtypeStruct((ROWS, 6 * WIDTH), BF16),
        in_specs=[vmem] * 6,
        out_specs=vmem,
        scratch_shapes=[
            pltpu.VMEM((8, 2, UNIT, WIDTH), BF16),
            pltpu.VMEM((2, 2, 16, HALF, WIDTH), BF16),
            pltpu.VMEM((2, 2, HALF, WIDTH), BF16),
            pltpu.VMEM((2, 2, 16, HALF, WIDTH), F32),
            pltpu.VMEM((8, 2, 512, WIDTH), F32),
            pltpu.VMEM((4, 2, 512, WIDTH), BF16),
            pltpu.VMEM((4, 2, 512, WIDTH), BF16),
            pltpu.VMEM((4, 512, WIDTH), BF16),
            pltpu.VMEM((4, 512, WIDTH), BF16),
            pltpu.VMEM((4, 512, WIDTH), BF16),
            pltpu.VMEM((4, 512, WIDTH), BF16),
            pltpu.VMEM((2, 3, 4, 2, HALF, WIDTH), BF16),
            pltpu.VMEM((2, 3, 4, 2, HALF, WIDTH), BF16),
            pltpu.VMEM((2, 4, 2, HALF, WIDTH), BF16),
            pltpu.VMEM((2, 4, 2, HALF, WIDTH), BF16),
            dma((4, 2)), dma((4, 2)), dma((2, 2)), dma((2, 2)), dma((4, 2)), dma((4, 2)),
            dma((2, 4)), dma((2, 4)), dma((2, 3, 4)), dma((2, 3, 4)),
            dma((4,)), dma((4,)), dma((4,)), dma((4,)), dma((4,)), dma((4,)),
            dma((2, 3, 4)), dma((2, 3, 4)), dma((2, 4)), dma((2, 4)),
        ],
        compiler_params=pltpu.CompilerParams(
            collective_id=0, has_side_effects=True, vmem_limit_bytes=56 * 2**20
        ),
    )(queries, key_rows, value_rows, forward_out, out_grad, log_norm.T)
    return pl.pallas_call(
        part,
        name="part",
        out_shape=(
            jax.ShapeDtypeStruct(queries.shape, BF16),
            jax.ShapeDtypeStruct(key_rows.shape, BF16),
            jax.ShapeDtypeStruct(value_rows.shape, BF16),
        ),
        in_specs=[vmem],
        out_specs=(vmem,) * 3,
    )(whole)


def solution(mesh):
    placed = P(("outer", "inner"), None)
    return jax.shard_map(
        local,
        mesh=mesh,
        in_specs=(placed,) * 6,
        out_specs=(placed,) * 3,
        check_vma=False,
    )
```
